32 devices in a mesh: ctx: 8 (over z, y), head: 4 (over x, core).
Axes of the slice: x: 2, y: 2, z: 4, core: 2. Of those that a mesh axis runs over, the one named last changes fastest.
Arguments:
- entries: bfloat16 [16384, 2048], P('ctx', 'head'), may hold values from -6 to 6
- gating: bfloat16 [16384, 2048], P('ctx', 'head'), may hold values from -6 to 6
- state_in: bfloat16 [16384, 128], P('ctx'), may hold values from -2 to 2
- state_out: bfloat16 [16384, 128], P('ctx'), may hold values from -2 to 2
- step_size: float32 [32, 16384], P('head', 'ctx'), may hold values from 0.2 to 1.5
- decay_rate: float32 [32], P('head'), may hold values from 6.1035157e-06 to 0.1
- skip_gain: float32 [32], P('head'), may hold values from 0.5 to 1.5
- level_gate: float32 [32, 5, 16384], P('head', None, 'ctx'), may hold values from 0.2 to 1.5
- norm_gain: float32 [2048], P('head'), may hold values from 0.5 to 1.5
- cotangent: bfloat16 [16384, 2048], P('ctx'), may hold values from -0.119628906 to 0.119628906
- master_weight: float32 [2048, 2048], P('ctx', 'head'), may hold values from -0.125 to 0.125
- first_moment: float32 [2048, 2048], P('ctx', 'head'), may hold values from -3 to 3
- second_moment: float32 [2048, 2048], P('ctx', 'head'), may hold values from 0.1 to 10
Outputs:
- normed: bfloat16 [16384, 2048], P('ctx', 'head')
- weights: bfloat16 [2048, 2048], P(None, 'head')
- gradient: float32 [2048, 2048], P('ctx', 'head')
The draws below stay inside these ranges and needn't reach their ends.
All inputs are finite; a program needn't handle non-finite values.
Results may differ from the reference program's by a relative error of at most 0.0059.
Values may be sent and summed in bfloat16 or wider, within the bound.
No kernel may reach another device: no remote copies, remote signals or barrier semaphores. Data moves between devices by JAX's collectives and lax.ppermute only.
A program may use at most 128 MiB of HBM per device.

```python
import math
import jax
import jax.numpy as jnp
from jax import lax

D = 2048
HEADS = 32
HEAD_DIM = 64
STATE = 128
TOK_DEV = 2048
BLOCK = 256
LEVELS = 5
INNER = 2048
TOKENS = 16384
N_CTX = 8


def block_scale(key, extent, shards, least, top_value):
    def one(axis_at, blocks):
        steps = jax.random.uniform(jax.random.fold_in(jax.random.fold_in(key, 6), axis_at), (blocks,), jnp.float32, least / len(shards), top_value / len(shards))
        return jnp.repeat(jnp.exp(steps), extent[axis_at] // blocks).reshape((-1,) + (1,) * (len(extent) - axis_at - 1))

    gain = one(*shards[0])
    for cut in shards[1:]:
        gain = gain * one(*cut)
    return gain


def gaussian(key, extent, spread, limit, split=(), kind=jnp.bfloat16):
    factor_of = block_scale(key, extent, split, -0.22, 0.18) if split else 1.0
    drawn = jax.random.normal(key, extent, jnp.float32) * spread * factor_of
    return jnp.minimum(jnp.maximum(drawn, -limit), limit).astype(kind)


def setup_inputs(seed: int = 0) -> dict:
    arg_keys = jax.random.split(jax.random.key(seed), 14)
    return {
        "entries": gaussian(arg_keys[0], (TOKENS, INNER), 1.0, 6.0, ((0, 8), (1, 4))),
        "gating": gaussian(arg_keys[1], (TOKENS, INNER), 1.0, 6.0, ((0, 8), (1, 4))),
        "state_in": gaussian(arg_keys[2], (TOKENS, STATE), 0.3, 2.0, ((0, 8),)),
        "state_out": gaussian(arg_keys[3], (TOKENS, STATE), 0.3, 2.0, ((0, 8),)),
        "step_size": jnp.clip(0.2 + 1.3 * jax.random.uniform(arg_keys[4], (HEADS, TOKENS), jnp.float32) ** block_scale(arg_keys[4], (HEADS, TOKENS), ((0, 4), (1, 8)), -0.2, 0.2), 0.2, 1.5),
        "decay_rate": jnp.clip(jnp.exp(math.log(0.1) - 9.704061 * jax.random.uniform(arg_keys[5], (HEADS,), jnp.float32) ** block_scale(arg_keys[5], (HEADS,), ((0, 4),), -0.2, 0.2)), 6.10351571594947e-06, 0.1),
        "skip_gain": jnp.clip(0.5 + 1.0 * jax.random.uniform(arg_keys[6], (HEADS,), jnp.float32) ** block_scale(arg_keys[6], (HEADS,), ((0, 4),), -0.2, 0.2), 0.5, 1.5),
        "level_gate": jnp.clip(0.2 + 1.3 * jax.random.uniform(arg_keys[7], (HEADS, LEVELS, TOKENS), jnp.float32) ** block_scale(arg_keys[7], (HEADS, LEVELS, TOKENS), ((0, 4), (2, 8)), -0.2, 0.2), 0.2, 1.5),
        "norm_gain": jnp.clip(1.0 + 0.1 * jax.random.normal(arg_keys[8], (INNER,), jnp.float32), 0.5, 1.5),
        "cotangent": gaussian(arg_keys[9], (TOKENS, D), 0.02, 0.119628906, ((0, 8),)),
        "master_weight": gaussian(arg_keys[10], (D, INNER), INNER ** -0.5, 0.125, ((0, 8), (1, 4)), jnp.float32),
        "first_moment": gaussian(arg_keys[11], (D, INNER), 0.5, 3.0, ((0, 8), (1, 4)), jnp.float32),
        "second_moment": jnp.clip(jnp.exp(math.log(10.0) - 4.6051702 * jax.random.uniform(arg_keys[12], (D, INNER), jnp.float32) ** block_scale(arg_keys[12], (D, INNER), ((0, 8), (1, 4)), -0.2, 0.2)), 0.1, 10.0),
    }


def rounded(values):
    return lax.optimization_barrier(values.astype(jnp.bfloat16)).astype(jnp.float32)

def block_scan(scaled, state_in, state_out, log_decay):
    length, head_count, head_width = scaled.shape
    state_width = state_in.shape[1]
    blocks = length // BLOCK
    decay_blocks = log_decay.reshape(head_count, blocks, BLOCK).transpose(1, 0, 2)
    value_blocks = scaled.reshape(blocks, BLOCK, head_count, head_width)
    in_blocks = state_in.reshape(blocks, BLOCK, state_width)
    out_blocks = state_out.reshape(blocks, BLOCK, state_width)
    causal = jnp.arange(BLOCK)[:, None] >= jnp.arange(BLOCK)[None, :]

    def advance(running, pieces):
        decays, value_block, in_block, out_block = pieces
        prefix = jnp.cumsum(decays, axis=-1)
        scores = jnp.dot(out_block, in_block.T, preferred_element_type=jnp.float32)
        gap_matrix = jnp.where(causal[None], prefix[:, :, None] - prefix[:, None, :], 0.0)
        decay_mask = jnp.where(causal[None], jnp.exp(gap_matrix), 0.0)
        mix = (scores[None] * decay_mask).astype(jnp.bfloat16)
        within = jnp.einsum('hts,shp->thp', mix.astype(jnp.float32), value_block.astype(jnp.float32))
        carried = jnp.einsum('tn,hpn->thp', out_block.astype(jnp.float32), rounded(running))
        carried = carried * jnp.exp(prefix).T[:, :, None]
        to_end = (value_block.astype(jnp.float32) * jnp.exp(prefix[:, -1:] - prefix).T[:, :, None]).astype(jnp.bfloat16)
        update = jnp.einsum('thp,tn->hpn', to_end.astype(jnp.float32), in_block.astype(jnp.float32))
        running = jnp.exp(prefix[:, -1])[:, None, None] * running + update
        return (running, (within + carried, prefix))
    start = jnp.zeros((head_count, head_width, state_width), jnp.float32)
    end_state, (outputs, prefixes) = lax.scan(advance, start, (decay_blocks, value_blocks, in_blocks, out_blocks))
    totals = prefixes[:, :, -1]
    offsets = jnp.cumsum(totals, axis=0) - totals
    cumulative = (prefixes + offsets[:, :, None]).transpose(1, 0, 2).reshape(head_count, length)
    return (outputs.reshape(length, head_count, head_width), end_state, cumulative)

def level_states(all_ends, all_totals, position, depth):
    members = all_ends.shape[0]
    positions = jnp.arange(members, dtype=jnp.int32)
    between = (positions[None, :] > positions[:, None]) & (positions[None, :] < position)
    gap_decay = lax.optimization_barrier(jnp.sum(jnp.where(between[:, :, None], all_totals[None, :, :], 0.0), axis=1))
    collected = []
    for rung in range(depth):
        selected = (positions < position) & (jnp.right_shift(positions, rung + 1) == jnp.right_shift(position, rung + 1))
        selected = selected & (jnp.bitwise_and(jnp.right_shift(position, rung), 1) == 1)
        selected = selected & (jnp.bitwise_and(jnp.right_shift(positions, rung), 1) == 0)
        factor = jnp.where(selected[:, None], jnp.exp(gap_decay), 0.0)
        collected.append(jnp.einsum('jh,jhpn->hpn', factor, all_ends, precision=lax.Precision.HIGHEST))
    return collected

def finish(within, cumulative, by_head, gating, state_out, gate_rows, skip_gain, levels):
    length, head_count, head_width = within.shape
    across = jnp.zeros_like(within)
    for rung, level_state in enumerate(levels):
        readout = jnp.einsum('tn,hpn->thp', state_out.astype(jnp.float32), rounded(level_state))
        across = across + readout * gate_rows[:, rung, :].T[:, :, None]
    mixed = within + across * jnp.exp(cumulative).T[:, :, None] + skip_gain[None, :, None] * by_head.astype(jnp.float32)
    return mixed.reshape(length, head_count * head_width) * jax.nn.silu(gating.astype(jnp.float32))

def adamw(gradient, master, moment_one, moment_two):
    moment_one = 0.9 * moment_one + 0.1 * gradient
    moment_two = 0.95 * moment_two + 0.05 * gradient * gradient
    ratio = moment_one / (1.0 - 0.9 ** 10) / (jnp.sqrt(moment_two / (1.0 - 0.95 ** 10)) + 1e-08)
    return (master - 0.1 * (ratio + 0.1 * master)).astype(jnp.bfloat16)

def reference(entries, gating, state_in, state_out, step_size, decay_rate, skip_gain, level_gate, norm_gain, cotangent, master_weight, first_moment, second_moment):
    members = N_CTX
    depth = members.bit_length() - 1
    seg_entries = entries.reshape(members, TOK_DEV, HEADS, HEAD_DIM)
    seg_in = state_in.reshape(members, TOK_DEV, STATE)
    seg_out = state_out.reshape(members, TOK_DEV, STATE)
    seg_steps = step_size.reshape(HEADS, members, TOK_DEV).transpose(1, 0, 2)

    def local_pass(arrays):
        part_x, part_in, part_out, part_steps = arrays
        log_decay = -decay_rate[:, None] * part_steps
        scaled = (part_x.astype(jnp.float32) * part_steps.T[:, :, None]).astype(jnp.bfloat16)
        return block_scan(scaled, part_in, part_out, log_decay)
    withins, all_ends, cumulatives = lax.map(local_pass, (seg_entries, seg_in, seg_out, seg_steps))
    all_totals = cumulatives[:, :, -1]
    seg_gating = gating.reshape(members, TOK_DEV, INNER)
    seg_gate = level_gate.reshape(HEADS, LEVELS, members, TOK_DEV).transpose(2, 0, 1, 3)

    def output_pass(arrays):
        position, part_within, part_cum, part_x, part_z, part_out, part_gate = arrays
        levels = level_states(all_ends, all_totals, position, depth)
        gated = finish(part_within, part_cum, part_x, part_z, part_out, part_gate, skip_gain, levels)
        mean_sq = lax.optimization_barrier(jnp.sum(gated * gated, axis=1)) / INNER
        return (gated * lax.rsqrt(mean_sq + 1e-05)[:, None] * norm_gain[None, :]).astype(jnp.bfloat16)
    normed = lax.map(output_pass, (jnp.arange(members, dtype=jnp.int32), withins, cumulatives, seg_entries, seg_gating, seg_out, seg_gate))
    normed = normed.reshape(TOKENS, INNER)
    gradient = lax.dot_general(cotangent, normed, (((0,), (0,)), ((), ())), preferred_element_type=jnp.float32)
    weights = adamw(gradient, master_weight, first_moment, second_moment)
    return (normed, weights, gradient)
```

```python
import functools

import jax
import jax.numpy as jnp
from jax import lax
from jax.experimental import pallas as pl
from jax.experimental.pallas import tpu as pltpu
from jax.sharding import PartitionSpec as P

HEAD_DIM = 64
BLOCK = 256
BF16 = jnp.bfloat16
F32 = jnp.float32
VMEM_LIMIT = 48 * 1024 * 1024
TRANSPOSED_LHS = (((0,), (0,)), ((), ()))
TRANSPOSED_RHS = (((1,), (1,)), ((), ()))


def mm(a, b, dims=(((1,), (0,)), ((), ()))):
    return lax.dot_general(a, b, dims, preferred_element_type=F32)


def split(values):
    high = values.astype(BF16)
    return high, (values - high.astype(F32)).astype(BF16)


def params(steps=1):
    return pltpu.CompilerParams(
        dimension_semantics=("arbitrary",) * steps, vmem_limit_bytes=VMEM_LIMIT
    )


def head_select(heads, width):
    lane = lax.broadcasted_iota(jnp.int32, (heads, width), 1)
    row = lax.broadcasted_iota(jnp.int32, (heads, width), 0)
    return lane // (width // heads) == row


def spread_tokens(values, width):
    select = jnp.where(head_select(values.shape[0], width), 1.0, 0.0).astype(BF16)
    high, low = split(values.T)
    return mm(high, select) + mm(low, select)


def spread_row(values, width):
    heads = values.shape[0]
    return jnp.sum(jnp.where(head_select(heads, width), values, 0.0), axis=0, keepdims=True)


def prefix_sum(values):
    tokens = values.shape[1]
    row = lax.broadcasted_iota(jnp.int32, (tokens, tokens), 0)
    col = lax.broadcasted_iota(jnp.int32, (tokens, tokens), 1)
    upper = jnp.where(row <= col, 1.0, 0.0).astype(BF16)
    first, rest = split(values)
    second = (values - first.astype(F32) - rest.astype(F32)).astype(BF16)
    return mm(first, upper) + mm(rest, upper) + mm(second, upper)


def states_kernel(
    x_ref, b_ref, dt_ref, rate_ref, before_ref, prefix_ref, cum_ref, end_ref, decay_ref, pay_ref,
    run_ref, off_ref
):
    step = pl.program_id(0)
    width = x_ref.shape[1]

    @pl.when(step == 0)
    def _():
        run_ref[...] = jnp.zeros_like(run_ref)
        off_ref[...] = jnp.zeros_like(off_ref)

    before_ref[0] = run_ref[...].astype(BF16)
    steps = dt_ref[...]
    prefix = prefix_sum(-rate_ref[...] * steps)
    prefix_ref[...] = prefix
    cum_ref[...] = prefix + off_ref[:, 0:1]
    last = prefix[:, BLOCK - 1:BLOCK]
    weight = spread_tokens(steps * jnp.exp(last - prefix), width)
    scaled = (x_ref[...].astype(F32) * weight).astype(BF16)
    update = mm(b_ref[...], scaled, TRANSPOSED_LHS)
    running = spread_row(jnp.exp(last), width) * run_ref[...] + update
    run_ref[...] = running
    off_ref[...] = off_ref[...] + last

    @pl.when(step == pl.num_programs(0) - 1)
    def _():
        total = spread_row(off_ref[:, 0:1], width)
        end_ref[...] = running
        decay_ref[...] = total
        pack(pay_ref, running, total)


def pack(pay_ref, state, decay):
    rows = state.shape[0]
    first, second = split(decay)
    third = (decay - first.astype(F32) - second.astype(F32)).astype(BF16)
    row = lax.broadcasted_iota(jnp.int32, (16, state.shape[1]), 0)
    tail = jnp.where(
        row == 0,
        first.astype(F32),
        jnp.where(row == 1, second.astype(F32), jnp.where(row == 2, third.astype(F32), 0.0)),
    )
    pay_ref[0:rows] = state.astype(BF16)
    pay_ref[rows:rows + 16] = tail.astype(BF16)


def segment_states(entries, state_in, step_size, rate):
    length, width = entries.shape
    heads = rate.shape[0]
    states = state_in.shape[1]
    blocks = length // BLOCK
    whole = lambda shape: pl.BlockSpec(shape, lambda i: (0,) * len(shape))
    return pl.pallas_call(
        states_kernel,
        grid=(blocks,),
        in_specs=[
            pl.BlockSpec((BLOCK, width), lambda i: (i, 0)),
            pl.BlockSpec((BLOCK, states), lambda i: (i, 0)),
            pl.BlockSpec((heads, BLOCK), lambda i: (0, i)),
            whole((heads, 1)),
        ],
        out_specs=[
            pl.BlockSpec((1, states, width), lambda i: (i, 0, 0)),
            pl.BlockSpec((heads, BLOCK), lambda i: (0, i)),
            pl.BlockSpec((heads, BLOCK), lambda i: (0, i)),
            whole((states, width)),
            whole((1, width)),
            whole((states + 16, width)),
        ],
        out_shape=[
            jax.ShapeDtypeStruct((blocks, states, width), BF16),
            jax.ShapeDtypeStruct((heads, length), F32),
            jax.ShapeDtypeStruct((heads, length), F32),
            jax.ShapeDtypeStruct((states, width), F32),
            jax.ShapeDtypeStruct((1, width), F32),
            jax.ShapeDtypeStruct((states + 16, width), BF16),
        ],
        scratch_shapes=[pltpu.VMEM((states, width), F32), pltpu.VMEM((heads, 128), F32)],
        compiler_params=params(),
        name="segment_states",
    )(entries, state_in, step_size, rate)


def join_kernel(pos_ref, bit, got_ref, group_ref, decay_ref, before_ref,
                level_ref, group_out, decay_out, before_out, pay_ref):
    rows = group_ref.shape[0]
    upper = ((pos_ref[0] >> bit) & 1) == 1
    other = got_ref[0:rows].astype(F32)
    tail = got_ref[rows:rows + 16].astype(F32)
    other_decay = tail[0:1] + tail[1:2] + tail[2:3]
    decay = decay_ref[...]
    before = before_ref[...]
    group = group_ref[...]
    level_ref[...] = jnp.where(upper, jnp.exp(before) * other, 0.0).astype(BF16)
    joined = jnp.where(
        upper, group + jnp.exp(decay) * other, other + jnp.exp(other_decay) * group
    )
    group_out[...] = joined
    total = decay + other_decay
    decay_out[...] = total
    before_out[...] = jnp.where(upper, before + other_decay, before)
    pack(pay_ref, joined, total)


def join(position, bit, got, group, decay, before):
    full = lambda a: pl.BlockSpec(memory_space=pltpu.VMEM)
    row = jax.ShapeDtypeStruct(decay.shape, F32)
    return pl.pallas_call(
        lambda pos_ref, *refs: join_kernel(pos_ref, bit, *refs),
        in_specs=[pl.BlockSpec(memory_space=pltpu.SMEM)] + [full(a) for a in (got, group, decay, before)],
        out_specs=[pl.BlockSpec(memory_space=pltpu.VMEM)] * 5,
        out_shape=[
            jax.ShapeDtypeStruct(group.shape, BF16),
            jax.ShapeDtypeStruct(group.shape, F32),
            row,
            row,
            jax.ShapeDtypeStruct(got.shape, BF16),
        ],
        compiler_params=pltpu.CompilerParams(vmem_limit_bytes=VMEM_LIMIT),
        name="join_groups",
    )(position, got, group, decay, before)


def within_kernel(x_ref, z_ref, b_ref, c_ref, dt_ref, prefix_ref, state_ref, skip_ref, out_ref):
    width = x_ref.shape[1]
    prefix = prefix_ref[...]
    x = x_ref[...].astype(F32)
    weighted = (x * spread_tokens(dt_ref[...] * jnp.exp(-prefix), width)).astype(BF16)
    scores = mm(c_ref[...], b_ref[...], TRANSPOSED_RHS)
    row = lax.broadcasted_iota(jnp.int32, scores.shape, 0)
    col = lax.broadcasted_iota(jnp.int32, scores.shape, 1)
    high, low = split(jnp.where(col <= row, scores, 0.0))
    total = mm(high, weighted) + mm(low, weighted) + mm(c_ref[...], state_ref[0])
    total = total * spread_tokens(jnp.exp(prefix), width) + spread_row(skip_ref[...], width) * x
    z = z_ref[...].astype(F32)
    out_ref[...] = total * (z / (1.0 + jnp.exp(-z)))


def within_blocks(entries, gating, state_in, state_out, step_size, prefix, states, skip):
    length, width = entries.shape
    heads = skip.shape[0]
    state = state_in.shape[1]
    by_rows = lambda cols: pl.BlockSpec((BLOCK, cols), lambda i: (i, 0))
    by_cols = pl.BlockSpec((heads, BLOCK), lambda i: (0, i))
    return pl.pallas_call(
        within_kernel,
        grid=(length // BLOCK,),
        in_specs=[
            by_rows(width),
            by_rows(width),
            by_rows(state),
            by_rows(state),
            by_cols,
            by_cols,
            pl.BlockSpec((1, state, width), lambda i: (i, 0, 0)),
            pl.BlockSpec((heads, 1), lambda i: (0, 0)),
        ],
        out_specs=by_rows(width),
        out_shape=jax.ShapeDtypeStruct((length, width), F32),
        compiler_params=params(),
        name="within_blocks",
    )(entries, gating, state_in, state_out, step_size, prefix, states, skip)


def across_kernel(depth, base_ref, z_ref, c_ref, gate_ref, cum_ref, *refs):
    level_refs, (gated_ref, sums_ref) = refs[:depth], refs[depth:]
    width = base_ref.shape[1]
    decayed = jnp.exp(cum_ref[...])
    total = jnp.zeros(base_ref.shape, F32)
    for rung, level_ref in enumerate(level_refs):
        readout = mm(c_ref[...], level_ref[...])
        total = total + readout * spread_tokens(gate_ref[:, rung, :] * decayed, width)
    z = z_ref[...].astype(F32)
    gated = base_ref[...] + total * (z / (1.0 + jnp.exp(-z)))
    gated_ref[...] = gated
    high, low = split(gated * gated)
    ones = jnp.ones((8, width), BF16)
    sums = mm(ones, high, TRANSPOSED_RHS) + mm(ones, low, TRANSPOSED_RHS)
    sums_ref[...] = sums[0:1]


def across_levels(base, gating, state_out, level_gate, cumulative, levels):
    length, width = base.shape
    heads, rungs = level_gate.shape[:2]
    state = state_out.shape[1]
    by_rows = lambda cols: pl.BlockSpec((BLOCK, cols), lambda i: (i, 0))
    return pl.pallas_call(
        functools.partial(across_kernel, len(levels)),
        grid=(length // BLOCK,),
        in_specs=[
            by_rows(width),
            by_rows(width),
            by_rows(state),
            pl.BlockSpec((heads, rungs, BLOCK), lambda i: (0, 0, i)),
            pl.BlockSpec((heads, BLOCK), lambda i: (0, i)),
        ]
        + [pl.BlockSpec((state, width), lambda i: (0, 0))] * len(levels),
        out_specs=[by_rows(width), pl.BlockSpec((1, BLOCK), lambda i: (0, i))],
        out_shape=[
            jax.ShapeDtypeStruct((length, width), F32),
            jax.ShapeDtypeStruct((1, length), F32),
        ],
        compiler_params=params(),
        name="across_levels",
    )(base, gating, state_out, level_gate, cumulative, *levels)


def gradient_kernel(channels, gated_ref, sums_ref, gain_ref, cot_ref, normed_ref, out_ref, acc_ref):
    step = pl.program_id(0)
    inverse = lax.rsqrt(sums_ref[...] / channels + 1e-05)
    column = jnp.broadcast_to(inverse, (8, inverse.shape[1])).T[:, 0:1]
    normed = (gated_ref[...] * column * gain_ref[...]).astype(BF16)
    normed_ref[...] = normed

    @pl.when(step == 0)
    def _():
        acc_ref[...] = mm(cot_ref[...], normed, TRANSPOSED_LHS)

    @pl.when(step > 0)
    def _():
        acc_ref[...] += mm(cot_ref[...], normed, TRANSPOSED_LHS)

    @pl.when(step == pl.num_programs(0) - 1)
    def _():
        out_ref[...] = acc_ref[...]


def norm_gradient(gated, sums, gain, cotangent, channels):
    length, width = gated.shape
    rows = cotangent.shape[1]
    return pl.pallas_call(
        functools.partial(gradient_kernel, channels),
        grid=(length // BLOCK,),
        in_specs=[
            pl.BlockSpec((BLOCK, width), lambda i: (i, 0)),
            pl.BlockSpec((1, BLOCK), lambda i: (0, i)),
            pl.BlockSpec((1, width), lambda i: (0, 0)),
            pl.BlockSpec((BLOCK, rows), lambda i: (i, 0)),
        ],
        out_specs=[
            pl.BlockSpec((BLOCK, width), lambda i: (i, 0)),
            pl.BlockSpec((rows, width), lambda i: (0, 0)),
        ],
        out_shape=[
            jax.ShapeDtypeStruct((length, width), BF16),
            jax.ShapeDtypeStruct((rows, width), F32),
        ],
        scratch_shapes=[pltpu.VMEM((rows, width), F32)],
        compiler_params=params(),
        name="norm_gradient",
    )(gated, sums, gain, cotangent)


def adamw(gradient, master, moment_one, moment_two):
    moment_one = 0.9 * moment_one + 0.1 * gradient
    moment_two = 0.95 * moment_two + 0.05 * gradient * gradient
    ratio = moment_one / (1.0 - 0.9**10) / (jnp.sqrt(moment_two / (1.0 - 0.95**10)) + 1e-08)
    return (master - 0.1 * (ratio + 0.1 * master)).astype(BF16)


def flipped(block, axis, bit):
    count = lax.axis_size(axis)
    return lax.ppermute(block, axis, [(i, i ^ (1 << bit)) for i in range(count)])


def scatter_sum(terms, position, order):
    depth = len(order)
    left = list(range(depth - 1, -1, -1))
    for bit in order:
        axis = left.index(bit)
        left.pop(axis)
        mine = (position >> bit) & 1
        keep = lax.dynamic_index_in_dim(terms, mine, axis, keepdims=False).astype(F32)
        send = lax.dynamic_index_in_dim(terms, 1 - mine, axis, keepdims=False).astype(BF16)
        terms = keep + flipped(send, "ctx", bit).astype(F32)
    return terms


def gather_blocks(block, position, order):
    have = []
    for bit in reversed(order):
        other = flipped(block, "ctx", bit)
        axis = sum(1 for b in have if b > bit)
        mine = (position >> bit) & 1
        low = jnp.where(mine == 0, block, other)
        high = jnp.where(mine == 0, other, block)
        block = jnp.stack([low, high], axis=axis)
        have.append(bit)
    return block


def on_device(
    entries,
    gating,
    state_in,
    state_out,
    step_size,
    decay_rate,
    skip_gain,
    level_gate,
    norm_gain,
    cotangent,
    master_weight,
    first_moment,
    second_moment,
):
    width = entries.shape[1]
    channels = width * lax.axis_size("head")
    count = lax.axis_size("ctx")
    depth = count.bit_length() - 1
    position = lax.axis_index("ctx")
    rate = decay_rate[:, None]
    before_block, prefix, cumulative, group, decay, payload = segment_states(
        entries, state_in, step_size, rate
    )
    before = jnp.zeros_like(decay)
    where = position.astype(jnp.int32).reshape(1)
    levels = []
    for bit in range(depth):
        got = flipped(payload, "ctx", bit)
        level, group, decay, before, payload = join(where, bit, got, group, decay, before)
        levels.append(level)
    base = within_blocks(
        entries, gating, state_in, state_out, step_size, prefix, before_block, skip_gain[:, None]
    )
    gated, sums = across_levels(base, gating, state_out, level_gate, cumulative, levels)
    sums = jnp.sum(lax.all_gather(sums, "head", axis=0, tiled=False), axis=0)
    normed, terms = norm_gradient(gated, sums, norm_gain[None, :], cotangent, channels)

    rows = master_weight.shape[0]
    chunk = rows // 2
    terms = terms.reshape((2,) * depth + (2, chunk, width))
    bits = list(range(depth))
    orders = [bits, [1, 0] + bits[2:]]
    gradients, updates = [], []
    for half, order in enumerate(orders):
        part = slice(half * chunk, (half + 1) * chunk)
        summed = scatter_sum(terms[..., half, :, :], position, order)
        gradients.append(summed)
        updated = adamw(summed, master_weight[part], first_moment[part], second_moment[part])
        updates.append(gather_blocks(updated, position, order).reshape(count, chunk, width))
    gradient = jnp.concatenate(gradients, axis=0)
    weights = jnp.stack(updates, axis=1).reshape(count * rows, width)
    return (normed, weights, gradient)


def solution(mesh):
    return jax.shard_map(
        on_device,
        mesh=mesh,
        in_specs=(
            P("ctx", "head"),
            P("ctx", "head"),
            P("ctx", None),
            P("ctx", None),
            P("head", "ctx"),
            P("head"),
            P("head"),
            P("head", None, "ctx"),
            P("head"),
            P("ctx", None),
            P("ctx", "head"),
            P("ctx", "head"),
            P("ctx", "head"),
        ),
        out_specs=(P("ctx", "head"), P(None, "head"), P("ctx", "head")),
        check_vma=False,
    )
```

```python
import functools

import jax
import jax.numpy as jnp
from jax import lax
from jax.experimental import pallas as pl
from jax.experimental.pallas import tpu as pltpu
from jax.sharding import PartitionSpec as P

HEAD_DIM = 64
BLOCK = 256
BF16 = jnp.bfloat16
F32 = jnp.float32
MIB = 1024 * 1024
CUTS = (0, 4, 8)
PARTS = len(CUTS) - 1
TRANSPOSED_LHS = (((0,), (0,)), ((), ()))
TRANSPOSED_RHS = (((1,), (1,)), ((), ()))


def mm(a, b, dims=(((1,), (0,)), ((), ()))):
    return lax.dot_general(a, b, dims, preferred_element_type=F32)


def split(values):
    high = values.astype(BF16)
    return high, (values - high.astype(F32)).astype(BF16)


def params(mib, steps=1):
    return pltpu.CompilerParams(
        dimension_semantics=("arbitrary",) * steps, vmem_limit_bytes=mib * MIB
    )


def in_hbm(*arrays):
    return [pltpu.with_memory_space_constraint(array, pltpu.HBM) for array in arrays]


def in_vmem(*arrays):
    return [pltpu.with_memory_space_constraint(array, pltpu.VMEM) for array in arrays]


def turn_blocks(values):
    blocks = values.shape[1] // BLOCK
    return jnp.concatenate([values[:, i * BLOCK:(i + 1) * BLOCK] for i in range(blocks)], axis=0)


def prefix_sums(values):
    heads, tokens = values.shape
    rows = turn_blocks(values)
    row = lax.broadcasted_iota(jnp.int32, (BLOCK, BLOCK), 0)
    col = lax.broadcasted_iota(jnp.int32, (BLOCK, BLOCK), 1)
    upper = jnp.where(row <= col, 1.0, 0.0).astype(BF16)
    first, rest = split(rows)
    last = (rows - first.astype(F32) - rest.astype(F32)).astype(BF16)
    sums = mm(jnp.concatenate([first, rest, last], axis=0), upper)
    count = rows.shape[0]
    sums = sums[0:count] + sums[count:2 * count] + sums[2 * count:3 * count]
    return [sums[i * heads:(i + 1) * heads] for i in range(tokens // BLOCK)]


def as_column(row):
    heads = row.shape[1]
    diagonal = lax.broadcasted_iota(jnp.int32, (heads, heads), 0) == lax.broadcasted_iota(
        jnp.int32, (heads, heads), 1
    )
    return jnp.sum(jnp.where(diagonal, row, 0.0), axis=1, keepdims=True)


def head_rows(head):
    return slice(head * HEAD_DIM, (head + 1) * HEAD_DIM)


def states_kernel(
    x_ref, b_ref, dt_ref, rate_ref, before_ref, prefix_ref, cum_ref, end_ref, decay_ref, pay_ref,
    run_ref, off_ref
):
    step = pl.program_id(0)
    tokens, width = x_ref.shape
    states = b_ref.shape[1]
    heads = dt_ref.shape[0]

    @pl.when(step == 0)
    def _():
        run_ref[...] = jnp.zeros_like(run_ref)
        off_ref[...] = jnp.zeros_like(off_ref)

    offset = off_ref[:, 0:1]
    rate = as_column(rate_ref[...])
    for block, prefix in enumerate(prefix_sums(-rate * dt_ref[...])):
        part = slice(block * BLOCK, (block + 1) * BLOCK)
        prefix_ref[:, part] = prefix
        cum_ref[:, part] = prefix + offset
        last = prefix[:, BLOCK - 1:BLOCK]
        weight = jnp.exp(last - prefix)
        decay = jnp.broadcast_to(jnp.exp(last), (heads, states))
        steps = dt_ref[:, part]
        turned = x_ref[part].T
        pieces = []
        for head in range(heads):
            x = turned[head_rows(head)].astype(F32)
            scaled = (x * steps[head:head + 1]).astype(BF16).astype(F32)
            pieces.append((scaled * weight[head:head + 1]).astype(BF16))
        update = mm(jnp.concatenate(pieces, axis=0), b_ref[part])
        for head in range(heads):
            rows = head_rows(head)
            running = run_ref[rows]
            before_ref[block, rows] = running.astype(BF16)
            run_ref[rows] = decay[head:head + 1] * running + update[rows]
        offset = offset + last
    off_ref[...] = jnp.broadcast_to(offset, off_ref.shape)

    @pl.when(step == pl.num_programs(0) - 1)
    def _():
        total = jnp.broadcast_to(offset, (heads, states))
        end_ref[...] = run_ref[...]
        decay_ref[...] = total
        pay_ref[0:width] = run_ref[...].astype(BF16)
        first, second = split(total)
        third = (total - first.astype(F32) - second.astype(F32)).astype(BF16)
        terms = [first.astype(F32), second.astype(F32), third.astype(F32)]
        terms += [jnp.zeros_like(total)] * (tail_rows(heads) // heads - 3)
        pay_ref[width:] = jnp.concatenate(terms, axis=0).astype(BF16)


def tail_rows(heads):
    return -(-3 * heads // 16) * 16


def segment_states(entries, state_in, step_size, rate, tile=1024):
    length, width = entries.shape
    heads = rate.shape[1]
    states = state_in.shape[1]
    tile = min(tile, length)
    whole = lambda shape: pl.BlockSpec(shape, lambda i: (0,) * len(shape))
    return pl.pallas_call(
        states_kernel,
        grid=(length // tile,),
        in_specs=[
            pl.BlockSpec((tile, width), lambda i: (i, 0)),
            pl.BlockSpec((tile, states), lambda i: (i, 0)),
            pl.BlockSpec((heads, tile), lambda i: (0, i)),
            whole((1, heads)),
        ],
        out_specs=[
            pl.BlockSpec((tile // BLOCK, width, states), lambda i: (i, 0, 0)),
            pl.BlockSpec((heads, tile), lambda i: (0, i)),
            pl.BlockSpec((heads, tile), lambda i: (0, i)),
            whole((width, states)),
            whole((heads, states)),
            whole((width + tail_rows(heads), states)),
        ],
        out_shape=[
            pltpu.VMEM((length // BLOCK, width, states), BF16),
            pltpu.VMEM((heads, length), F32),
            pltpu.VMEM((heads, length), F32),
            jax.ShapeDtypeStruct((width, states), F32),
            jax.ShapeDtypeStruct((heads, states), F32),
            jax.ShapeDtypeStruct((width + tail_rows(heads), states), BF16),
        ],
        scratch_shapes=[pltpu.VMEM((width, states), F32), pltpu.VMEM((heads, 128), F32)],
        compiler_params=params(24),
        name="segment_states",
    )(*in_hbm(entries, state_in, step_size, rate))


def packed(state, decay):
    heads = decay.shape[0]
    first, second = split(decay)
    third = (decay - first.astype(F32) - second.astype(F32)).astype(BF16)
    spare = jnp.zeros((tail_rows(heads) - 3 * heads, decay.shape[1]), BF16)
    return jnp.concatenate([state.astype(BF16), first, second, third, spare], axis=0)


def unpacked(got, heads):
    width = got.shape[0] - tail_rows(heads)
    terms = got[width:width + 3 * heads].astype(F32).reshape(3, heads, got.shape[1])
    return got[0:width].astype(F32), terms[0] + terms[1] + terms[2]


def decayed(decay, state):
    heads, states = decay.shape
    return (jnp.exp(decay)[:, None, :] * state.reshape(heads, -1, states)).reshape(state.shape)


def joined(upper, state, decay, other, other_decay):
    both = jnp.where(
        upper, state + decayed(decay, other), other + decayed(other_decay, state)
    )
    return both, decay + other_decay


def level_of(upper, before, other, other_decay):
    level = jnp.where(upper, decayed(before, other), 0.0).astype(BF16)
    return level, jnp.where(upper, before + other_decay, before)


def level_states(payload, state, decay, position, depth, beside):
    heads = decay.shape[0]
    uppers = [((position >> bit) & 1) == 1 for bit in range(depth)]
    before = jnp.zeros_like(decay)
    levels = []
    near = min(depth, 2)
    got = [flipped(payload, "ctx", mask) for mask in range(1, 1 << near)]
    *got, beside = lax.optimization_barrier((*got, beside))
    got = [unpacked(each, heads) for each in got]
    for bit in range(depth):
        if bit == 0:
            other, other_decay = got[0]
        elif bit == 1:
            other, other_decay = joined(uppers[0], *got[1], *got[2])
        else:
            other, other_decay = unpacked(flipped(packed(state, decay), "ctx", 1 << bit), heads)
        level, before_next = level_of(uppers[bit], before, other, other_decay)
        levels.append(level)
        state, decay = joined(uppers[bit], state, decay, other, other_decay)
        before = before_next
    return levels, beside


def silu(z):
    return z * (0.5 + 0.5 * jnp.tanh(0.5 * z))


def within_kernel(
    x_ref, z_ref, b_ref, c_ref, dt_ref, prefix_ref, state_ref, skip_ref, base_ref, gating_ref
):
    tokens, width = x_ref.shape
    heads = dt_ref.shape[0]
    skip = jnp.broadcast_to(as_column(skip_ref[...]), (heads, BLOCK))
    row = lax.broadcasted_iota(jnp.int32, (BLOCK, BLOCK), 0)
    col = lax.broadcasted_iota(jnp.int32, (BLOCK, BLOCK), 1)
    for block in range(tokens // BLOCK):
        part = slice(block * BLOCK, (block + 1) * BLOCK)
        prefix = prefix_ref[:, part]
        grow, shrink = jnp.exp(-prefix), jnp.exp(prefix)
        steps = dt_ref[:, part]
        readout = c_ref[part]
        scores = mm(b_ref[part], readout, TRANSPOSED_RHS)
        high, low = split(jnp.where(row <= col, scores, 0.0))
        turned = x_ref[part].T
        highs, lows = [], []
        for head in range(heads):
            x = turned[head_rows(head)].astype(F32)
            scaled = (x * steps[head:head + 1]).astype(BF16).astype(F32)
            weighted, rest = split(scaled * grow[head:head + 1])
            highs.append(weighted)
            lows.append(rest)
        weighted, rest = jnp.concatenate(highs, axis=0), jnp.concatenate(lows, axis=0)
        total = mm(
            jnp.concatenate([weighted, weighted, rest], axis=1),
            jnp.concatenate([high, low, high], axis=0),
        ) + mm(state_ref[block], readout, TRANSPOSED_RHS)
        z_turned = z_ref[part].T
        gating_ref[:, part] = z_turned
        for head in range(heads):
            rows = head_rows(head)
            x = turned[rows].astype(F32)
            mixed = total[rows] * shrink[head:head + 1] + skip[head:head + 1] * x
            base_ref[rows, part] = (mixed * silu(z_turned[rows].astype(F32))).astype(BF16)


def within_blocks(entries, gating, state_in, state_out, step_size, prefix, states, skip, tile=512):
    length, width = entries.shape
    heads = skip.shape[1]
    state = state_in.shape[1]
    tile = min(tile, length)
    by_rows = lambda cols: pl.BlockSpec((tile, cols), lambda i: (i, 0))
    by_cols = lambda rows: pl.BlockSpec((rows, tile), lambda i: (0, i))
    return pl.pallas_call(
        within_kernel,
        grid=(length // tile,),
        in_specs=[
            by_rows(width),
            by_rows(width),
            by_rows(state),
            by_rows(state),
            by_cols(heads),
            by_cols(heads),
            pl.BlockSpec((tile // BLOCK, width, state), lambda i: (i, 0, 0)),
            pl.BlockSpec((1, heads), lambda i: (0, 0)),
        ],
        out_specs=[by_cols(width), by_cols(width)],
        out_shape=[
            pltpu.VMEM((width, length), BF16),
            pltpu.HBM((width, length), BF16),
        ],
        compiler_params=params(24),
        name="within_blocks",
    )(
        *in_hbm(entries, gating, state_in, state_out, step_size),
        *in_vmem(prefix, states),
        *in_hbm(skip),
    )


def across_kernel(depth, base_ref, z_ref, c_ref, gate_ref, cum_ref, *refs):
    level_refs, (gated_ref, sums_ref) = refs[:depth], refs[depth:]
    width, tokens = base_ref.shape
    heads = cum_ref.shape[0]
    per_pair = 128 // HEAD_DIM
    for block in range(tokens // BLOCK):
        part = slice(block * BLOCK, (block + 1) * BLOCK)
        decayed = jnp.exp(cum_ref[:, part])
        gates = [gate_ref[rung, :, part] * decayed for rung in range(depth)]
        readouts = [mm(level_ref[...], c_ref[part], TRANSPOSED_RHS) for level_ref in level_refs]
        squares = jnp.zeros((HEAD_DIM, BLOCK), F32)
        for first in range(0, heads, per_pair):
            pair = []
            for head in range(first, first + per_pair):
                rows = head_rows(head)
                total = jnp.zeros((HEAD_DIM, BLOCK), F32)
                for gate, readout in zip(gates, readouts):
                    total = total + readout[rows] * gate[head:head + 1]
                gated = base_ref[rows, part].astype(F32) + total * silu(z_ref[rows, part].astype(F32))
                squares = squares + gated * gated
                pair.append(gated)
            cols = slice(first * HEAD_DIM, (first + per_pair) * HEAD_DIM)
            gated_ref[part, cols] = jnp.concatenate(pair, axis=0).T.astype(BF16)
        sums_ref[:, part] = jnp.sum(squares, axis=0, keepdims=True)


def across_levels(base, gating, state_out, level_gate, cumulative, levels, tile=512):
    width, length = base.shape
    rungs, heads = level_gate.shape[:2]
    state = state_out.shape[1]
    tile = min(tile, length)
    by_cols = lambda rows: pl.BlockSpec((rows, tile), lambda i: (0, i))
    return pl.pallas_call(
        functools.partial(across_kernel, len(levels)),
        grid=(length // tile,),
        in_specs=[
            by_cols(width),
            by_cols(width),
            pl.BlockSpec((tile, state), lambda i: (i, 0)),
            pl.BlockSpec((rungs, heads, tile), lambda i: (0, 0, i)),
            by_cols(heads),
        ]
        + [pl.BlockSpec((width, state), lambda i: (0, 0))] * len(levels),
        out_specs=[pl.BlockSpec((tile, width), lambda i: (i, 0)), by_cols(1)],
        out_shape=[
            pltpu.VMEM((length, width), BF16),
            jax.ShapeDtypeStruct((1, length), F32),
        ],
        compiler_params=params(24),
        name="across_levels",
    )(
        *in_vmem(base),
        *in_hbm(gating, state_out, level_gate),
        *in_vmem(cumulative),
        *levels,
    )


def normalize(channels, gated_ref, sums_ref, gain_ref, normed_ref):
    for block in range(gated_ref.shape[0] // BLOCK):
        part = slice(block * BLOCK, (block + 1) * BLOCK)
        inverse = lax.rsqrt(jnp.sum(sums_ref[:, part], axis=0, keepdims=True) / channels + 1e-05)
        column = jnp.broadcast_to(inverse, (8, BLOCK)).T[:, 0:1]
        normed_ref[part] = (gated_ref[part].astype(F32) * column * gain_ref[...]).astype(BF16)


def gradient_kernel(channels, gated_ref, sums_ref, gain_ref, cot_ref, normed_ref, out_ref):
    @pl.when(pl.program_id(0) == 0)
    def _():
        normalize(channels, gated_ref, sums_ref, gain_ref, normed_ref)

    out_ref[...] = mm(cot_ref[...], normed_ref[...], TRANSPOSED_LHS)


def norm_gradient(gated, sums, gain, cotangent, channels, tile=512):
    length, width = gated.shape
    rows = cotangent.shape[1]
    whole = lambda shape: pl.BlockSpec(shape, lambda i: (0,) * len(shape))
    return pl.pallas_call(
        functools.partial(gradient_kernel, channels),
        grid=(rows // tile,),
        in_specs=[
            whole((length, width)),
            whole(sums.shape),
            whole((1, width)),
            pl.BlockSpec((length, tile), lambda i: (0, i)),
        ],
        out_specs=[whole((length, width)), pl.BlockSpec((tile, width), lambda i: (i, 0))],
        out_shape=[
            jax.ShapeDtypeStruct((length, width), BF16),
            jax.ShapeDtypeStruct((rows, width), F32),
        ],
        compiler_params=params(32),
        name="norm_gradient",
    )(*in_vmem(gated), sums, gain, *in_hbm(cotangent))


def masks_of(bits):
    masks = [0]
    for bit in reversed(bits):
        masks = masks + [mask | 1 << bit for mask in masks]
    return masks


def column_specs(orders, length, count, chunk, keep):
    def spec(slot):
        def index(half, pos_ref):
            flips = [masks_of(order[1:])[slot] | (0 if keep else 1 << order[0]) for order in orders]
            flip = jnp.where(half == 0, flips[0], flips[1])
            return (0, 2 * (pos_ref[0] ^ flip) + half)

        return pl.BlockSpec((length, chunk), index)

    return [spec(slot) for slot in range(count // 2)]


def part_slices(width):
    edges = [cut * width // 8 for cut in CUTS]
    return [slice(start, stop) for start, stop in zip(edges, edges[1:])]


def store_half(product, out_refs):
    for half in range(2):

        @pl.when(pl.program_id(0) == half)
        def _():
            for part, cols in enumerate(part_slices(product.shape[1])):
                out_ref = out_refs[2 * part + half]
                out_ref[...] = product[:, cols].reshape(out_ref.shape).astype(out_ref.dtype)


def send_kernel(channels, pos_ref, gated_ref, sums_ref, gain_ref, *refs):
    cot_refs, (normed_ref, *out_refs) = refs[:-2 * PARTS - 1], refs[-2 * PARTS - 1:]

    @pl.when(pl.program_id(0) == 0)
    def _():
        normalize(channels, gated_ref, sums_ref, gain_ref, normed_ref)

    columns = jnp.concatenate([ref[...] for ref in cot_refs], axis=1)
    store_half(mm(columns, normed_ref[...], TRANSPOSED_LHS), out_refs)


def keep_kernel(pos_ref, normed_ref, *refs):
    cot_refs, out_refs = refs[:-2 * PARTS], refs[-2 * PARTS:]
    columns = jnp.concatenate([ref[...] for ref in cot_refs], axis=1)
    store_half(mm(columns, normed_ref[...], TRANSPOSED_LHS), out_refs)


def terms_call(kernel, name, position, inputs, cotangent, orders, chunk, keep, outs, dtype):
    length, width = inputs[0].shape
    count = 1 << len(orders[0])
    cots = column_specs(orders, length, count, chunk, keep)
    whole = lambda shape: pl.BlockSpec(shape, lambda i, pos_ref: (0,) * len(shape))
    shapes = [
        (count // 2, chunk, cols.stop - cols.start) for cols in part_slices(width) for _ in range(2)
    ]
    out = pl.pallas_call(
        kernel,
        grid_spec=pltpu.PrefetchScalarGridSpec(
            num_scalar_prefetch=1,
            grid=(2,),
            in_specs=[whole(each.shape) for each in inputs] + cots,
            out_specs=[whole(each.shape) for each in outs] + [whole(shape) for shape in shapes],
        ),
        out_shape=outs + [jax.ShapeDtypeStruct(shape, dtype) for shape in shapes],
        compiler_params=params(32),
        name=name,
    )(position, *inputs, *in_hbm(*[cotangent] * len(cots)))
    terms = out[len(outs):]
    return out[:len(outs)], [terms[2 * part:2 * part + 2] for part in range(PARTS)]


def terms_to_send(position, gated, sums, gain, cotangent, channels, orders, chunk):
    return terms_call(
        functools.partial(send_kernel, channels),
        "terms_to_send",
        position,
        [*in_vmem(gated), sums, gain],
        cotangent,
        orders,
        chunk,
        False,
        [pltpu.HBM(gated.shape, BF16)],
        BF16,
    )


def terms_to_keep(position, normed, cotangent, orders, chunk):
    return terms_call(
        keep_kernel,
        "terms_to_keep",
        position,
        in_hbm(normed),
        cotangent,
        orders,
        chunk,
        True,
        [],
        F32,
    )[1]


def place_kernel(slots, rows, pos_ref, *refs):
    block_refs, (out_ref, sems) = refs[:-2], refs[-2:]
    copies = []
    for block_ref, (masks, half, start) in zip(block_refs, slots):
        _, chunk, width = block_ref.shape
        for slot, mask in enumerate(masks):
            row = pl.multiple_of((pos_ref[0] ^ mask) * rows + half * chunk, chunk)
            target = out_ref.at[pl.ds(row, chunk), pl.ds(start, width)]
            copies.append(
                pltpu.make_async_copy(block_ref.at[slot], target, sems.at[len(copies)])
            )
    for copy in copies:
        copy.start()
    for copy in copies:
        copy.wait()


def placed(position, pieces, shape, rows):
    blocks = [block for block, *_ in pieces]
    slots = [tuple(place) for _, *place in pieces]
    return pl.pallas_call(
        functools.partial(place_kernel, slots, rows),
        in_specs=[pl.BlockSpec(memory_space=pltpu.SMEM)]
        + [pl.BlockSpec(memory_space=pltpu.VMEM)] * len(blocks),
        out_specs=pl.BlockSpec(memory_space=pltpu.HBM),
        out_shape=jax.ShapeDtypeStruct(shape, BF16),
        scratch_shapes=[pltpu.SemaphoreType.DMA((sum(len(masks) for masks, *_ in slots),))],
        compiler_params=pltpu.CompilerParams(vmem_limit_bytes=16 * MIB),
        name="placed_weights",
    )(position, *blocks)


def adamw(gradient, master, moment_one, moment_two):
    moment_one = 0.9 * moment_one + 0.1 * gradient
    moment_two = 0.95 * moment_two + 0.05 * gradient * gradient
    ratio = moment_one / (1.0 - 0.9**10) / (jnp.sqrt(moment_two / (1.0 - 0.95**10)) + 1e-08)
    return (master - 0.1 * (ratio + 0.1 * master)).astype(BF16)


def flipped(block, axis, mask):
    count = lax.axis_size(axis)
    return lax.ppermute(block, axis, [(i, i ^ mask) for i in range(count)])


def fold(total, bit):
    slots = total.shape[0] // 2
    got = flipped(total[slots:].astype(BF16), "ctx", 1 << bit)
    return total[:slots] + got.astype(F32)


def gathered(have, masks, orders, start):
    chunk = have.shape[1] // 2
    pieces = []
    for half, order in enumerate(orders):
        mine = have[:, half * chunk:(half + 1) * chunk]
        names = masks
        for bit in reversed(order[1:2]):
            mine = jnp.concatenate([mine, flipped(mine, "ctx", 1 << bit)], axis=0)
            names = names + [mask | 1 << bit for mask in names]
        last = flipped(mine, "ctx", 1 << order[0])
        pieces.append((mine, names, half, start))
        pieces.append((last, [mask | 1 << order[0] for mask in names], half, start))
    return pieces


def on_device(
    entries,
    gating,
    state_in,
    state_out,
    step_size,
    decay_rate,
    skip_gain,
    level_gate,
    norm_gain,
    cotangent,
    master_weight,
    first_moment,
    second_moment,
):
    width = entries.shape[1]
    channels = width * lax.axis_size("head")
    count = lax.axis_size("ctx")
    depth = count.bit_length() - 1
    position = lax.axis_index("ctx")
    before_block, prefix, cumulative, group, decay, payload = segment_states(
        entries, state_in, step_size, decay_rate[None, :]
    )
    base, turned = within_blocks(
        entries, gating, state_in, state_out, step_size, prefix, before_block, skip_gain[None, :]
    )
    levels, (base, turned) = level_states(
        payload, group, decay, position, depth, (base, turned)
    )
    gates = level_gate.transpose(1, 0, 2)
    gated, sums = across_levels(base, turned, state_out, gates, cumulative, levels)
    sums = lax.all_gather(sums[0], "head", axis=0, tiled=False)

    rows = master_weight.shape[0]
    chunk = rows // 2
    parts = part_slices(width)
    gain = norm_gain[None, :]
    bits = list(range(depth))
    orders = [bits, [1, 0] + bits[2:]]
    where = position.astype(jnp.int32).reshape(1)
    sends, keeps = [], []
    if chunk % 128 == 0:
        (normed,), sends = terms_to_send(
            where, gated, sums, gain, cotangent, channels, orders, chunk
        )
        keeps = terms_to_keep(where, normed, cotangent, orders, chunk)
    else:
        normed, terms = norm_gradient(gated, sums, gain, cotangent, channels)
        terms = terms.reshape(count, 2, chunk, width)
        for cols in parts:
            for kind, flip, dtype in ((sends, 1, BF16), (keeps, 0, F32)):
                kind.append([
                    terms[position ^ jnp.array(masks_of(order[1:])) ^ (flip << order[0])][
                        :, half, :, cols
                    ].astype(dtype)
                    for half, order in enumerate(orders)
                ])
    gots = [
        [flipped(term, "ctx", 1 << order[0]) for term, order in zip(send, orders)]
        for send in sends
    ]
    totals = []
    for keep, got in zip(keeps, gots):
        halves = []
        for mine, other, order in zip(keep, got, orders):
            total = mine + other.astype(F32)
            for bit in order[1:2]:
                total = fold(total, bit)
            halves.append(total)
        totals.append(jnp.concatenate(halves, axis=1))
    for bit in bits[2:]:
        totals = [fold(total, bit) for total in totals]
    gradients = [total[0] for total in totals]
    haves = [
        adamw(total, master_weight[:, cols], first_moment[:, cols], second_moment[:, cols])[None]
        for total, cols in zip(gradients, parts)
    ]
    masks = [0]
    for bit in reversed(bits[2:]):
        haves = [
            jnp.concatenate([have, flipped(have, "ctx", 1 << bit)], axis=0) for have in haves
        ]
        masks = masks + [mask | 1 << bit for mask in masks]
    pieces = []
    for have, cols in zip(haves, parts):
        pieces += gathered(have, masks, orders, cols.start)
    gradient = jnp.concatenate(gradients, axis=1)
    weights = placed(where, pieces, (count * rows, width), rows)
    return (normed, weights, gradient)


def solution(mesh):
    return jax.shard_map(
        on_device,
        mesh=mesh,
        in_specs=(
            P("ctx", "head"),
            P("ctx", "head"),
            P("ctx", None),
            P("ctx", None),
            P("head", "ctx"),
            P("head"),
            P("head"),
            P("head", None, "ctx"),
            P("head"),
            P("ctx", None),
            P("ctx", "head"),
            P("ctx", "head"),
            P("ctx", "head"),
        ),
        out_specs=(P("ctx", "head"), P(None, "head"), P("ctx", "head")),
        check_vma=False,
    )
```

```python
import functools

import jax
import jax.numpy as jnp
from jax import lax
from jax.experimental import pallas as pl
from jax.experimental.pallas import tpu as pltpu
from jax.sharding import PartitionSpec as P

HEAD_DIM = 64
BLOCK = 256
BF16 = jnp.bfloat16
F32 = jnp.float32
MIB = 1024 * 1024
TRANSPOSED_LHS = (((0,), (0,)), ((), ()))
TRANSPOSED_RHS = (((1,), (1,)), ((), ()))


def mm(a, b, dims=(((1,), (0,)), ((), ()))):
    return lax.dot_general(a, b, dims, preferred_element_type=F32)


def split(values):
    high = values.astype(BF16)
    return high, (values - high.astype(F32)).astype(BF16)


def params(mib, steps=1):
    return pltpu.CompilerParams(
        dimension_semantics=("arbitrary",) * steps, vmem_limit_bytes=mib * MIB
    )


def in_hbm(*arrays):
    return [pltpu.with_memory_space_constraint(array, pltpu.HBM) for array in arrays]


def in_vmem(*arrays):
    return [pltpu.with_memory_space_constraint(array, pltpu.VMEM) for array in arrays]


def turn_blocks(values):
    blocks = values.shape[1] // BLOCK
    return jnp.concatenate([values[:, i * BLOCK:(i + 1) * BLOCK] for i in range(blocks)], axis=0)


def prefix_sums(values):
    heads, tokens = values.shape
    rows = turn_blocks(values)
    row = lax.broadcasted_iota(jnp.int32, (BLOCK, BLOCK), 0)
    col = lax.broadcasted_iota(jnp.int32, (BLOCK, BLOCK), 1)
    upper = jnp.where(row <= col, 1.0, 0.0).astype(BF16)
    first, rest = split(rows)
    last = (rows - first.astype(F32) - rest.astype(F32)).astype(BF16)
    sums = mm(jnp.concatenate([first, rest, last], axis=0), upper)
    count = rows.shape[0]
    sums = sums[0:count] + sums[count:2 * count] + sums[2 * count:3 * count]
    return [sums[i * heads:(i + 1) * heads] for i in range(tokens // BLOCK)]


def as_column(row):
    heads = row.shape[1]
    diagonal = lax.broadcasted_iota(jnp.int32, (heads, heads), 0) == lax.broadcasted_iota(
        jnp.int32, (heads, heads), 1
    )
    return jnp.sum(jnp.where(diagonal, row, 0.0), axis=1, keepdims=True)


def head_rows(head):
    return slice(head * HEAD_DIM, (head + 1) * HEAD_DIM)


def states_kernel(
    x_ref, b_ref, dt_ref, rate_ref, before_ref, prefix_ref, cum_ref, end_ref, decay_ref, pay_ref,
    run_ref, off_ref
):
    step = pl.program_id(0)
    tokens, width = x_ref.shape
    states = b_ref.shape[1]
    heads = dt_ref.shape[0]

    @pl.when(step == 0)
    def _():
        run_ref[...] = jnp.zeros_like(run_ref)
        off_ref[...] = jnp.zeros_like(off_ref)

    offset = off_ref[:, 0:1]
    rate = as_column(rate_ref[...])
    for block, prefix in enumerate(prefix_sums(-rate * dt_ref[...])):
        part = slice(block * BLOCK, (block + 1) * BLOCK)
        prefix_ref[:, part] = prefix
        cum_ref[:, part] = prefix + offset
        last = prefix[:, BLOCK - 1:BLOCK]
        weight = jnp.exp(last - prefix)
        decay = jnp.broadcast_to(jnp.exp(last), (heads, states))
        steps = dt_ref[:, part]
        turned = x_ref[part].T
        pieces = []
        for head in range(heads):
            x = turned[head_rows(head)].astype(F32)
            scaled = (x * steps[head:head + 1]).astype(BF16).astype(F32)
            pieces.append((scaled * weight[head:head + 1]).astype(BF16))
        update = mm(jnp.concatenate(pieces, axis=0), b_ref[part])
        for head in range(heads):
            rows = head_rows(head)
            running = run_ref[rows]
            before_ref[block, rows] = running.astype(BF16)
            run_ref[rows] = decay[head:head + 1] * running + update[rows]
        offset = offset + last
    off_ref[...] = jnp.broadcast_to(offset, off_ref.shape)

    @pl.when(step == pl.num_programs(0) - 1)
    def _():
        total = jnp.broadcast_to(offset, (heads, states))
        end_ref[...] = run_ref[...]
        decay_ref[...] = total
        pay_ref[0:width] = run_ref[...].astype(BF16)
        pay_ref[width:] = packed_tail(total)


def tail_rows(heads):
    return -(-3 * heads // 16) * 16


def segment_states(entries, state_in, step_size, rate, tile=1024):
    length, width = entries.shape
    heads = rate.shape[1]
    states = state_in.shape[1]
    tile = min(tile, length)
    whole = lambda shape: pl.BlockSpec(shape, lambda i: (0,) * len(shape))
    return pl.pallas_call(
        states_kernel,
        grid=(length // tile,),
        in_specs=[
            pl.BlockSpec((tile, width), lambda i: (i, 0)),
            pl.BlockSpec((tile, states), lambda i: (i, 0)),
            pl.BlockSpec((heads, tile), lambda i: (0, i)),
            whole((1, heads)),
        ],
        out_specs=[
            pl.BlockSpec((tile // BLOCK, width, states), lambda i: (i, 0, 0)),
            pl.BlockSpec((heads, tile), lambda i: (0, i)),
            pl.BlockSpec((heads, tile), lambda i: (0, i)),
            whole((width, states)),
            whole((heads, states)),
            whole((width + tail_rows(heads), states)),
        ],
        out_shape=[
            pltpu.VMEM((length // BLOCK, width, states), BF16),
            pltpu.HBM((heads, length), F32),
            pltpu.HBM((heads, length), F32),
            jax.ShapeDtypeStruct((width, states), F32),
            jax.ShapeDtypeStruct((heads, states), F32),
            pltpu.VMEM((width + tail_rows(heads), states), BF16),
        ],
        scratch_shapes=[pltpu.VMEM((width, states), F32), pltpu.VMEM((heads, 128), F32)],
        compiler_params=params(24),
        name="segment_states",
    )(*in_hbm(entries, state_in, step_size, rate))


def packed(state, decay):
    heads = decay.shape[0]
    first, second = split(decay)
    third = (decay - first.astype(F32) - second.astype(F32)).astype(BF16)
    spare = jnp.zeros((tail_rows(heads) - 3 * heads, decay.shape[1]), BF16)
    return jnp.concatenate([state.astype(BF16), first, second, third, spare], axis=0)


def unpacked(got, heads):
    width = got.shape[0] - tail_rows(heads)
    terms = got[width:width + 3 * heads].astype(F32).reshape(3, heads, got.shape[1])
    return got[0:width].astype(F32), terms[0] + terms[1] + terms[2]


def decayed(decay, state):
    heads, states = decay.shape
    return (jnp.exp(decay)[:, None, :] * state.reshape(heads, -1, states)).reshape(state.shape)


def joined(upper, state, decay, other, other_decay):
    both = jnp.where(
        upper, state + decayed(decay, other), other + decayed(other_decay, state)
    )
    return both, decay + other_decay


def level_of(upper, before, other, other_decay):
    level = jnp.where(upper, decayed(before, other), 0.0).astype(BF16)
    return level, jnp.where(upper, before + other_decay, before)


def near_kernel(
    pos_ref, got_one, got_two, got_three, state_ref, decay_ref,
    low_ref, high_ref, pay_ref, group_ref, total_ref, before_ref
):
    heads = decay_ref.shape[0]
    width = state_ref.shape[0]
    odd = (pos_ref[0] & 1) == 1
    late = ((pos_ref[0] >> 1) & 1) == 1
    first = decay_ref[...]

    def tail(got):
        terms = got[width:].astype(F32)
        return terms[0:heads] + terms[heads:2 * heads] + terms[2 * heads:3 * heads]

    second, third, fourth = tail(got_one), tail(got_two), tail(got_three)
    before = jnp.where(odd, second, 0.0)
    own, other = first + second, third + fourth
    own_first = jnp.where(odd, 1.0, jnp.exp(second))
    own_second = jnp.where(odd, jnp.exp(first), 1.0)
    other_first = jnp.where(odd, 1.0, jnp.exp(fourth))
    other_second = jnp.where(odd, jnp.exp(third), 1.0)
    from_own = jnp.where(late, 1.0, jnp.exp(other))
    from_other = jnp.where(late, jnp.exp(own), 1.0)
    reach = jnp.exp(before)
    total = own + other
    for head in range(heads):
        rows, row = head_rows(head), slice(head, head + 1)
        one = got_one[rows].astype(F32)
        pair = own_first[row] * state_ref[rows] + own_second[row] * one
        far = other_first[row] * got_two[rows].astype(F32)
        far = far + other_second[row] * got_three[rows].astype(F32)
        low_ref[rows] = jnp.where(odd, one, 0.0).astype(BF16)
        high_ref[rows] = jnp.where(late, reach[row] * far, 0.0).astype(BF16)
        group = from_own[row] * pair + from_other[row] * far
        group_ref[rows] = group
        pay_ref[rows] = group.astype(BF16)
    pay_ref[width:] = packed_tail(total)
    total_ref[...] = total
    before_ref[...] = jnp.where(late, before + other, before)


def packed_tail(decay):
    heads = decay.shape[0]
    first, second = split(decay)
    third = (decay - first.astype(F32) - second.astype(F32)).astype(BF16)
    terms = [first.astype(F32), second.astype(F32), third.astype(F32)]
    terms += [jnp.zeros_like(decay)] * (tail_rows(heads) // heads - 3)
    return jnp.concatenate(terms, axis=0).astype(BF16)


def near_levels(where, gots, state, decay):
    width, states = state.shape
    own = lambda dtype: pltpu.VMEM((width, states), dtype)
    row = pltpu.VMEM(decay.shape, F32)
    return pl.pallas_call(
        near_kernel,
        in_specs=[pl.BlockSpec(memory_space=pltpu.SMEM)]
        + [pl.BlockSpec(memory_space=pltpu.VMEM)] * 5,
        out_specs=[pl.BlockSpec(memory_space=pltpu.VMEM)] * 6,
        out_shape=[own(BF16), own(BF16), pltpu.VMEM(gots[0].shape, BF16), own(F32), row, row],
        compiler_params=pltpu.CompilerParams(vmem_limit_bytes=16 * MIB),
        name="near_levels",
    )(where, *in_vmem(*gots, state, decay))


def level_states(payload, state, decay, position, depth, beside):
    heads = decay.shape[0]
    gots = [flipped(payload, "ctx", mask) for mask in (1, 2, 3)]
    *gots, beside = lax.optimization_barrier((*gots, beside))
    where = position.astype(jnp.int32).reshape(1)
    *levels, payload, state, decay, before = near_levels(where, gots, state, decay)
    for bit in range(2, depth):
        upper = ((position >> bit) & 1) == 1
        other, other_decay = unpacked(flipped(payload, "ctx", 1 << bit), heads)
        level, before = level_of(upper, before, other, other_decay)
        levels.append(level)
        if bit < depth - 1:
            state, decay = joined(upper, state, decay, other, other_decay)
            payload = packed(state, decay)
    return levels, beside


def silu(z):
    return z * (0.5 + 0.5 * jnp.tanh(0.5 * z))


def within_kernel(
    x_ref, z_ref, b_ref, c_ref, dt_ref, prefix_ref, state_ref, skip_ref, base_ref, gating_ref
):
    tokens, width = x_ref.shape
    heads = dt_ref.shape[0]
    skip = jnp.broadcast_to(as_column(skip_ref[...]), (heads, BLOCK))
    row = lax.broadcasted_iota(jnp.int32, (BLOCK, BLOCK), 0)
    col = lax.broadcasted_iota(jnp.int32, (BLOCK, BLOCK), 1)
    for block in range(tokens // BLOCK):
        part = slice(block * BLOCK, (block + 1) * BLOCK)
        prefix = prefix_ref[:, part]
        grow, shrink = jnp.exp(-prefix), jnp.exp(prefix)
        steps = dt_ref[:, part]
        readout = c_ref[part]
        scores = mm(b_ref[part], readout, TRANSPOSED_RHS)
        high, low = split(jnp.where(row <= col, scores, 0.0))
        turned = x_ref[part].T
        highs, lows = [], []
        for head in range(heads):
            x = turned[head_rows(head)].astype(F32)
            scaled = (x * steps[head:head + 1]).astype(BF16).astype(F32)
            weighted, rest = split(scaled * grow[head:head + 1])
            highs.append(weighted)
            lows.append(rest)
        weighted, rest = jnp.concatenate(highs, axis=0), jnp.concatenate(lows, axis=0)
        total = mm(
            jnp.concatenate([weighted, weighted, rest], axis=1),
            jnp.concatenate([high, low, high], axis=0),
        ) + mm(state_ref[block], readout, TRANSPOSED_RHS)
        z_turned = z_ref[part].T
        gating_ref[:, part] = z_turned
        for head in range(heads):
            rows = head_rows(head)
            x = turned[rows].astype(F32)
            mixed = total[rows] * shrink[head:head + 1] + skip[head:head + 1] * x
            base_ref[rows, part] = (mixed * silu(z_turned[rows].astype(F32))).astype(BF16)


def within_blocks(entries, gating, state_in, state_out, step_size, prefix, states, skip, tile=512):
    length, width = entries.shape
    heads = skip.shape[1]
    state = state_in.shape[1]
    tile = min(tile, length)
    by_rows = lambda cols: pl.BlockSpec((tile, cols), lambda i: (i, 0))
    by_cols = lambda rows: pl.BlockSpec((rows, tile), lambda i: (0, i))
    return pl.pallas_call(
        within_kernel,
        grid=(length // tile,),
        in_specs=[
            by_rows(width),
            by_rows(width),
            by_rows(state),
            by_rows(state),
            by_cols(heads),
            by_cols(heads),
            pl.BlockSpec((tile // BLOCK, width, state), lambda i: (i, 0, 0)),
            pl.BlockSpec((1, heads), lambda i: (0, 0)),
        ],
        out_specs=[by_cols(width), by_cols(width)],
        out_shape=[
            pltpu.VMEM((width, length), BF16),
            pltpu.HBM((width, length), BF16),
        ],
        compiler_params=params(24),
        name="within_blocks",
    )(
        *in_hbm(entries, gating, state_in, state_out, step_size, prefix),
        *in_vmem(states),
        *in_hbm(skip),
    )


def across_kernel(depth, base_ref, z_ref, c_ref, gate_ref, cum_ref, *refs):
    level_refs, (gated_ref, sums_ref) = refs[:depth], refs[depth:]
    width, tokens = base_ref.shape
    heads = cum_ref.shape[0]
    per_pair = 128 // HEAD_DIM
    for block in range(tokens // BLOCK):
        part = slice(block * BLOCK, (block + 1) * BLOCK)
        decayed = jnp.exp(cum_ref[:, part])
        gates = [gate_ref[rung, :, part] * decayed for rung in range(depth)]
        readouts = [mm(level_ref[...], c_ref[part], TRANSPOSED_RHS) for level_ref in level_refs]
        squares = jnp.zeros((HEAD_DIM, BLOCK), F32)
        for first in range(0, heads, per_pair):
            pair = []
            for head in range(first, first + per_pair):
                rows = head_rows(head)
                total = jnp.zeros((HEAD_DIM, BLOCK), F32)
                for gate, readout in zip(gates, readouts):
                    total = total + readout[rows] * gate[head:head + 1]
                gated = base_ref[rows, part].astype(F32) + total * silu(z_ref[rows, part].astype(F32))
                squares = squares + gated * gated
                pair.append(gated)
            cols = slice(first * HEAD_DIM, (first + per_pair) * HEAD_DIM)
            gated_ref[part, cols] = jnp.concatenate(pair, axis=0).T.astype(BF16)
        sums_ref[:, part] = jnp.sum(squares, axis=0, keepdims=True)


def across_levels(base, gating, state_out, level_gate, cumulative, levels, tile=1024):
    width, length = base.shape
    rungs, heads = level_gate.shape[:2]
    state = state_out.shape[1]
    tile = min(tile, length)
    by_cols = lambda rows: pl.BlockSpec((rows, tile), lambda i: (0, i))
    return pl.pallas_call(
        functools.partial(across_kernel, len(levels)),
        grid=(length // tile,),
        in_specs=[
            by_cols(width),
            by_cols(width),
            pl.BlockSpec((tile, state), lambda i: (i, 0)),
            pl.BlockSpec((rungs, heads, tile), lambda i: (0, 0, i)),
            by_cols(heads),
        ]
        + [pl.BlockSpec((width, state), lambda i: (0, 0))] * len(levels),
        out_specs=[pl.BlockSpec((tile, width), lambda i: (i, 0)), by_cols(1)],
        out_shape=[
            pltpu.VMEM((length, width), BF16),
            jax.ShapeDtypeStruct((1, length), F32),
        ],
        compiler_params=params(24),
        name="across_levels",
    )(
        *in_vmem(base),
        *in_hbm(gating, state_out, level_gate, cumulative),
        *levels,
    )


def normalize(channels, gated_ref, sums_ref, gain_ref, normed_ref):
    for block in range(gated_ref.shape[0] // BLOCK):
        part = slice(block * BLOCK, (block + 1) * BLOCK)
        inverse = lax.rsqrt(jnp.sum(sums_ref[:, part], axis=0, keepdims=True) / channels + 1e-05)
        column = jnp.broadcast_to(inverse, (8, BLOCK)).T[:, 0:1]
        normed_ref[part] = (gated_ref[part].astype(F32) * column * gain_ref[...]).astype(BF16)


def gradient_kernel(channels, gated_ref, sums_ref, gain_ref, cot_ref, normed_ref, out_ref):
    @pl.when(pl.program_id(0) == 0)
    def _():
        normalize(channels, gated_ref, sums_ref, gain_ref, normed_ref)

    out_ref[...] = mm(cot_ref[...], normed_ref[...], TRANSPOSED_LHS)


def norm_gradient(gated, sums, gain, cotangent, channels, tile=512):
    length, width = gated.shape
    rows = cotangent.shape[1]
    whole = lambda shape: pl.BlockSpec(shape, lambda i: (0,) * len(shape))
    return pl.pallas_call(
        functools.partial(gradient_kernel, channels),
        grid=(rows // tile,),
        in_specs=[
            whole((length, width)),
            whole(sums.shape),
            whole((1, width)),
            pl.BlockSpec((length, tile), lambda i: (0, i)),
        ],
        out_specs=[whole((length, width)), pl.BlockSpec((tile, width), lambda i: (i, 0))],
        out_shape=[
            jax.ShapeDtypeStruct((length, width), BF16),
            jax.ShapeDtypeStruct((rows, width), F32),
        ],
        compiler_params=params(32),
        name="norm_gradient",
    )(*in_vmem(gated), sums, gain, *in_hbm(cotangent))


def masks_of(bits):
    masks = [0]
    for bit in reversed(bits):
        masks = masks + [mask | 1 << bit for mask in masks]
    return masks


def slot_flips(order, kind, keep):
    later = masks_of(order[2:])
    later = later[:1] if kind == "near" else later[1:]
    first = 0 if keep else 1 << order[0]
    return [first | second | mask for second in (0, 1 << order[1]) for mask in later]


def column_specs(orders, jobs, tile, chunk):
    def spec(flip, half):
        return pl.BlockSpec(
            (tile, chunk), lambda i, pos_ref: (i, 2 * (pos_ref[0] ^ flip) + half)
        )

    return [
        spec(flip, half)
        for kind, keep in jobs
        for half, order in enumerate(orders)
        for flip in slot_flips(order, kind, keep)
    ]


def terms_kernel(channels, pos_ref, *refs):
    refs, acc_ref = refs[:-1], refs[-1]
    if channels is None:
        normed_ref, rest = refs[0], refs[1:]
    else:
        gated_ref, sums_ref, gain_ref, *rest = refs
    outs = [ref for ref in rest if len(ref.shape) == 3]
    rest = [ref for ref in rest if len(ref.shape) == 2]
    if channels is not None:
        normed_ref = rest.pop()
        normalize(channels, gated_ref, sums_ref, gain_ref, normed_ref)
    columns = jnp.concatenate([ref[...] for ref in rest], axis=1)
    product = mm(columns, normed_ref[...], TRANSPOSED_LHS)
    step, steps = pl.program_id(0), pl.num_programs(0)

    @pl.when(step == 0)
    def _():
        acc_ref[...] = product

    @pl.when((step > 0) & (step < steps - 1))
    def _():
        acc_ref[...] += product

    @pl.when(step == steps - 1)
    def _():
        start = 0
        for out_ref in outs:
            slots, chunk, _ = out_ref.shape
            rows = slice(start, start + slots * chunk)
            total = acc_ref[rows] + product[rows]
            out_ref[...] = total.reshape(out_ref.shape).astype(out_ref.dtype)
            start += slots * chunk


def terms_call(name, position, normed, cotangent, orders, jobs, chunk, norm=None, tile=1024):
    length, width = cotangent.shape[0], normed.shape[1]
    tile = min(tile, length // 2)
    cots = column_specs(orders, jobs, tile, chunk)
    shapes = [
        (len(slot_flips(order, kind, keep)), chunk, width)
        for kind, keep in jobs
        for order in orders
    ]
    dtypes = [F32 if keep else BF16 for _, keep in jobs for _ in orders]
    whole = lambda shape: pl.BlockSpec(shape, lambda i, pos_ref: (0,) * len(shape))
    by_tokens = pl.BlockSpec((tile, width), lambda i, pos_ref: (i, 0))
    in_specs, outs, out_specs, channels = [by_tokens], [], [], None
    if norm is None:
        inputs = in_hbm(normed)
    else:
        sums, gain, channels = norm
        inputs = [*in_vmem(normed), sums, gain]
        in_specs += [
            pl.BlockSpec((sums.shape[0], tile), lambda i, pos_ref: (0, i)),
            whole(gain.shape),
        ]
        outs, out_specs = [pltpu.HBM(normed.shape, BF16)], [by_tokens]
    result = pl.pallas_call(
        functools.partial(terms_kernel, channels),
        grid_spec=pltpu.PrefetchScalarGridSpec(
            num_scalar_prefetch=1,
            grid=(length // tile,),
            in_specs=in_specs + cots,
            out_specs=out_specs + [whole(shape) for shape in shapes],
            scratch_shapes=[pltpu.VMEM((len(cots) * chunk, width), F32)],
        ),
        out_shape=outs + [jax.ShapeDtypeStruct(*each) for each in zip(shapes, dtypes)],
        compiler_params=params(32),
        name=name,
    )(position, *inputs, *in_hbm(*[cotangent] * len(cots)))
    terms = result[len(outs):]
    return result[:len(outs)], [terms[2 * job:2 * job + 2] for job in range(len(jobs))]


def place_kernel(slots, rows, pos_ref, *refs):
    block_refs, (out_ref, sems) = refs[:len(slots)], refs[-2:]
    copies = []
    for block_ref, (masks, half) in zip(block_refs, slots):
        _, chunk, _ = block_ref.shape
        for slot, mask in enumerate(masks):
            row = pl.multiple_of((pos_ref[0] ^ mask) * rows + half * chunk, chunk)
            copies.append(
                pltpu.make_async_copy(
                    block_ref.at[slot], out_ref.at[pl.ds(row, chunk)], sems.at[len(copies)]
                )
            )
    for copy in copies:
        copy.start()
    for copy in copies:
        copy.wait()


def placed(position, pieces, shape, rows, name, already=None):
    blocks = [block for block, *_ in pieces]
    slots = [tuple(place) for _, *place in pieces]
    before = [] if already is None else [already]
    return pl.pallas_call(
        functools.partial(place_kernel, slots, rows),
        in_specs=[pl.BlockSpec(memory_space=pltpu.SMEM)]
        + [pl.BlockSpec(memory_space=pltpu.VMEM)] * len(blocks)
        + [pl.BlockSpec(memory_space=pltpu.HBM)] * len(before),
        out_specs=pl.BlockSpec(memory_space=pltpu.HBM),
        out_shape=pltpu.HBM(shape, BF16),
        scratch_shapes=[pltpu.SemaphoreType.DMA((sum(len(masks) for masks, *_ in slots),))],
        input_output_aliases={1 + len(blocks): 0} if before else {},
        compiler_params=pltpu.CompilerParams(vmem_limit_bytes=16 * MIB),
        name=name,
    )(position, *blocks, *before)


def adamw(gradient, master, moment_one, moment_two):
    moment_one = 0.9 * moment_one + 0.1 * gradient
    moment_two = 0.95 * moment_two + 0.05 * gradient * gradient
    ratio = moment_one / (1.0 - 0.9**10) / (jnp.sqrt(moment_two / (1.0 - 0.95**10)) + 1e-08)
    return (master - 0.1 * (ratio + 0.1 * master)).astype(BF16)


def update_kernel(keep_ref, got_ref, master_ref, one_ref, two_ref, gradient_ref, updated_ref):
    gradient = keep_ref[...] + got_ref[...].astype(F32)
    gradient_ref[...] = gradient
    updated_ref[...] = adamw(gradient, master_ref[...], one_ref[...], two_ref[...])


def update(keep, got, master, one, two):
    shape = keep.shape
    return pl.pallas_call(
        update_kernel,
        out_shape=[jax.ShapeDtypeStruct(shape, F32), jax.ShapeDtypeStruct(shape, BF16)],
        compiler_params=pltpu.CompilerParams(vmem_limit_bytes=16 * MIB),
        name="update_rows",
    )(keep, got, master, one, two)


def flipped(block, axis, mask):
    count = lax.axis_size(axis)
    return lax.ppermute(block, axis, [(i, i ^ mask) for i in range(count)])


def first_sums(keeps, sends, orders):
    sums = []
    for keep, send, order in zip(keeps, sends, orders):
        total = keep + flipped(send, "ctx", 1 << order[0]).astype(F32)
        slots = total.shape[0] // 2
        sums.append((total[slots:].astype(BF16), total[:slots]))
    return sums


def second_sums(sums, orders):
    halves = [
        keep + flipped(send, "ctx", 1 << order[1]).astype(F32)
        for (send, keep), order in zip(sums, orders)
    ]
    return jnp.concatenate(halves, axis=1)


def nearby(have, orders):
    chunk = have.shape[1] // 2
    halves = []
    for half, order in enumerate(orders):
        mine = have[:, half * chunk:(half + 1) * chunk]
        halves.append(jnp.concatenate([mine, flipped(mine, "ctx", 1 << order[1])], axis=0))
    return halves


def gathered(halves, masks, orders):
    pieces = []
    for half, order in enumerate(orders):
        names = masks + [mask | 1 << order[1] for mask in masks]
        last = flipped(halves[half], "ctx", 1 << order[0])
        pieces.append((halves[half], names, half))
        pieces.append((last, [mask | 1 << order[0] for mask in names], half))
    return pieces


def on_device(
    entries,
    gating,
    state_in,
    state_out,
    step_size,
    decay_rate,
    skip_gain,
    level_gate,
    norm_gain,
    cotangent,
    master_weight,
    first_moment,
    second_moment,
):
    width = entries.shape[1]
    channels = width * lax.axis_size("head")
    count = lax.axis_size("ctx")
    depth = count.bit_length() - 1
    position = lax.axis_index("ctx")
    before_block, prefix, cumulative, group, decay, payload = segment_states(
        entries, state_in, step_size, decay_rate[None, :]
    )
    base, turned = within_blocks(
        entries, gating, state_in, state_out, step_size, prefix, before_block, skip_gain[None, :]
    )
    levels, (base, turned) = level_states(
        payload, group, decay, position, depth, (base, turned)
    )
    gates = level_gate.transpose(1, 0, 2)
    gated, sums = across_levels(base, turned, state_out, gates, cumulative, levels)
    sums = lax.all_gather(sums[0], "head", axis=0, tiled=False)

    rows = master_weight.shape[0]
    chunk = rows // 2
    gain = norm_gain[None, :]
    bits = list(range(depth))
    orders = [bits, [1, 0] + bits[2:]]
    where = position.astype(jnp.int32).reshape(1)
    if chunk % 128 == 0:
        call = lambda name, normed, jobs, **kw: terms_call(
            name, where, normed, cotangent, orders, jobs, chunk, **kw
        )
        (normed,), (far_sends,) = call(
            "far_terms_to_send", gated, [("far", False)], norm=(sums, gain, channels)
        )
        _, (far_keeps, near_sends) = call(
            "far_terms_to_keep", normed, [("far", True), ("near", False)]
        )
        firsts = first_sums(far_keeps, far_sends, orders)
        firsts, near_sends = lax.optimization_barrier((firsts, near_sends))
        far = second_sums(firsts, orders)
        far, again = lax.optimization_barrier((far, normed))
        _, (near_keeps,) = call("near_terms_to_keep", again, [("near", True)])
    else:
        normed, terms = norm_gradient(gated, sums, gain, cotangent, channels)
        terms = terms.reshape(count, 2, chunk, width)
        pick = lambda kind, keep: [
            terms[position ^ jnp.array(slot_flips(order, kind, keep)), half].astype(
                F32 if keep else BF16
            )
            for half, order in enumerate(orders)
        ]
        far_sends, far_keeps = pick("far", False), pick("far", True)
        near_sends, near_keeps = pick("near", False), pick("near", True)
        far = second_sums(first_sums(far_keeps, far_sends, orders), orders)
    near = second_sums(first_sums(near_keeps, near_sends, orders), orders)
    totals = dict(zip(masks_of(bits[2:]), [near[0], *far]))
    for bit in bits[2:]:
        left = [mask for mask in totals if not mask >> bit & 1]
        send = jnp.stack([totals[mask | 1 << bit].astype(BF16) for mask in left])
        got = flipped(send, "ctx", 1 << bit)
        if bit == depth - 1:
            gradient, updated = update(
                totals[0], got[0], master_weight, first_moment, second_moment
            )
        totals = {mask: totals[mask] + got[at].astype(F32) for at, mask in enumerate(left)}
    halves = nearby(updated[None], orders)
    have, masks = updated[None], [0]
    for bit in reversed(bits[2:]):
        got = flipped(have, "ctx", 1 << bit)
        got = lax.optimization_barrier((got, halves[1]))[0]
        have = jnp.concatenate([have, got], axis=0)
        masks = masks + [mask | 1 << bit for mask in masks]
    pieces = gathered(halves, [0], orders)
    pieces += gathered(nearby(have[1:], orders), masks[1:], orders)
    shape = (count * rows, width)
    late = [pieces[5], pieces[7]]
    early = pieces[:5] + [pieces[6]]
    weights = placed(where, early, shape, rows, "placed_early")
    weights = placed(where, late, shape, rows, "placed_late", weights)
    return (normed, weights, gradient)


def solution(mesh):
    return jax.shard_map(
        on_device,
        mesh=mesh,
        in_specs=(
            P("ctx", "head"),
            P("ctx", "head"),
            P("ctx", None),
            P("ctx", None),
            P("head", "ctx"),
            P("head"),
            P("head"),
            P("head", None, "ctx"),
            P("head"),
            P("ctx", None),
            P("ctx", "head"),
            P("ctx", "head"),
            P("ctx", "head"),
        ),
        out_specs=(P("ctx", "head"), P(None, "head"), P("ctx", "head")),
        check_vma=False,
    )
```

```python
import functools

import jax
import jax.numpy as jnp
from jax import lax
from jax.experimental import pallas as pl
from jax.experimental.pallas import tpu as pltpu
from jax.sharding import PartitionSpec as P

HEAD_DIM = 64
BLOCK = 256
BF16 = jnp.bfloat16
F32 = jnp.float32
MIB = 1024 * 1024
TRANSPOSED_LHS = (((0,), (0,)), ((), ()))
TRANSPOSED_RHS = (((1,), (1,)), ((), ()))


def mm(a, b, dims=(((1,), (0,)), ((), ()))):
    return lax.dot_general(a, b, dims, preferred_element_type=F32)


def split(values):
    high = values.astype(BF16)
    return high, (values - high.astype(F32)).astype(BF16)


def params(mib, steps=1):
    return pltpu.CompilerParams(
        dimension_semantics=("arbitrary",) * steps, vmem_limit_bytes=mib * MIB
    )


def in_hbm(*arrays):
    return [pltpu.with_memory_space_constraint(array, pltpu.HBM) for array in arrays]


def in_vmem(*arrays):
    return [pltpu.with_memory_space_constraint(array, pltpu.VMEM) for array in arrays]


def turn_blocks(values):
    blocks = values.shape[1] // BLOCK
    return jnp.concatenate([values[:, i * BLOCK:(i + 1) * BLOCK] for i in range(blocks)], axis=0)


def prefix_sums(values):
    heads, tokens = values.shape
    rows = turn_blocks(values)
    row = lax.broadcasted_iota(jnp.int32, (BLOCK, BLOCK), 0)
    col = lax.broadcasted_iota(jnp.int32, (BLOCK, BLOCK), 1)
    upper = jnp.where(row <= col, 1.0, 0.0).astype(BF16)
    first, rest = split(rows)
    last = (rows - first.astype(F32) - rest.astype(F32)).astype(BF16)
    sums = mm(jnp.concatenate([first, rest, last], axis=0), upper)
    count = rows.shape[0]
    sums = sums[0:count] + sums[count:2 * count] + sums[2 * count:3 * count]
    return [sums[i * heads:(i + 1) * heads] for i in range(tokens // BLOCK)]


def as_column(row):
    heads = row.shape[1]
    diagonal = lax.broadcasted_iota(jnp.int32, (heads, heads), 0) == lax.broadcasted_iota(
        jnp.int32, (heads, heads), 1
    )
    return jnp.sum(jnp.where(diagonal, row, 0.0), axis=1, keepdims=True)


def head_rows(head):
    return slice(head * HEAD_DIM, (head + 1) * HEAD_DIM)


def states_kernel(
    x_ref, b_ref, dt_ref, rate_ref, before_ref, prefix_ref, cum_ref, end_ref, decay_ref, pay_ref,
    run_ref, off_ref
):
    step = pl.program_id(0)
    tokens, width = x_ref.shape
    states = b_ref.shape[1]
    heads = dt_ref.shape[0]

    @pl.when(step == 0)
    def _():
        run_ref[...] = jnp.zeros_like(run_ref)
        off_ref[...] = jnp.zeros_like(off_ref)

    offset = off_ref[:, 0:1]
    rate = as_column(rate_ref[...])
    for block, prefix in enumerate(prefix_sums(-rate * dt_ref[...])):
        part = slice(block * BLOCK, (block + 1) * BLOCK)
        prefix_ref[:, part] = prefix
        cum_ref[:, part] = prefix + offset
        last = prefix[:, BLOCK - 1:BLOCK]
        weight = jnp.exp(last - prefix)
        decay = jnp.broadcast_to(jnp.exp(last), (heads, states))
        steps = dt_ref[:, part]
        turned = x_ref[part].T
        pieces = []
        for head in range(heads):
            x = turned[head_rows(head)].astype(F32)
            scaled = (x * steps[head:head + 1]).astype(BF16).astype(F32)
            pieces.append((scaled * weight[head:head + 1]).astype(BF16))
        update = mm(jnp.concatenate(pieces, axis=0), b_ref[part])
        for head in range(heads):
            rows = head_rows(head)
            running = run_ref[rows]
            before_ref[block, rows] = running.astype(BF16)
            run_ref[rows] = decay[head:head + 1] * running + update[rows]
        offset = offset + last
    off_ref[...] = jnp.broadcast_to(offset, off_ref.shape)

    @pl.when(step == pl.num_programs(0) - 1)
    def _():
        total = jnp.broadcast_to(offset, (heads, states))
        end_ref[...] = run_ref[...]
        decay_ref[...] = total
        pay_ref[0:width] = run_ref[...].astype(BF16)
        pay_ref[width:] = packed_tail(total)


def tail_rows(heads):
    return -(-3 * heads // 16) * 16


def segment_states(entries, state_in, step_size, rate, tile=1024):
    length, width = entries.shape
    heads = rate.shape[1]
    states = state_in.shape[1]
    tile = min(tile, length)
    whole = lambda shape: pl.BlockSpec(shape, lambda i: (0,) * len(shape))
    return pl.pallas_call(
        states_kernel,
        grid=(length // tile,),
        in_specs=[
            pl.BlockSpec((tile, width), lambda i: (i, 0)),
            pl.BlockSpec((tile, states), lambda i: (i, 0)),
            pl.BlockSpec((heads, tile), lambda i: (0, i)),
            whole((1, heads)),
        ],
        out_specs=[
            pl.BlockSpec((tile // BLOCK, width, states), lambda i: (i, 0, 0)),
            pl.BlockSpec((heads, tile), lambda i: (0, i)),
            pl.BlockSpec((heads, tile), lambda i: (0, i)),
            whole((width, states)),
            whole((heads, states)),
            whole((width + tail_rows(heads), states)),
        ],
        out_shape=[
            pltpu.VMEM((length // BLOCK, width, states), BF16),
            pltpu.HBM((heads, length), F32),
            pltpu.HBM((heads, length), F32),
            jax.ShapeDtypeStruct((width, states), F32),
            jax.ShapeDtypeStruct((heads, states), F32),
            pltpu.VMEM((width + tail_rows(heads), states), BF16),
        ],
        scratch_shapes=[pltpu.VMEM((width, states), F32), pltpu.VMEM((heads, 128), F32)],
        compiler_params=params(24),
        name="segment_states",
    )(*in_hbm(entries, state_in, step_size, rate))


def packed(state, decay):
    heads = decay.shape[0]
    first, second = split(decay)
    third = (decay - first.astype(F32) - second.astype(F32)).astype(BF16)
    spare = jnp.zeros((tail_rows(heads) - 3 * heads, decay.shape[1]), BF16)
    return jnp.concatenate([state.astype(BF16), first, second, third, spare], axis=0)


def unpacked(got, heads):
    width = got.shape[0] - tail_rows(heads)
    terms = got[width:width + 3 * heads].astype(F32).reshape(3, heads, got.shape[1])
    return got[0:width].astype(F32), terms[0] + terms[1] + terms[2]


def decayed(decay, state):
    heads, states = decay.shape
    return (jnp.exp(decay)[:, None, :] * state.reshape(heads, -1, states)).reshape(state.shape)


def joined(upper, state, decay, other, other_decay):
    both = jnp.where(
        upper, state + decayed(decay, other), other + decayed(other_decay, state)
    )
    return both, decay + other_decay


def level_of(upper, before, other, other_decay):
    level = jnp.where(upper, decayed(before, other), 0.0).astype(BF16)
    return level, jnp.where(upper, before + other_decay, before)


def near_kernel(
    pos_ref, got_one, got_two, got_three, state_ref, decay_ref,
    low_ref, high_ref, pay_ref, before_ref, *group_refs
):
    heads = decay_ref.shape[0]
    width = state_ref.shape[0]
    odd = (pos_ref[0] & 1) == 1
    late = ((pos_ref[0] >> 1) & 1) == 1
    first = decay_ref[...]

    def tail(got):
        terms = got[width:].astype(F32)
        return terms[0:heads] + terms[heads:2 * heads] + terms[2 * heads:3 * heads]

    second, third, fourth = tail(got_one), tail(got_two), tail(got_three)
    before = jnp.where(odd, second, 0.0)
    own, other = first + second, third + fourth
    own_first = jnp.where(odd, 1.0, jnp.exp(second))
    own_second = jnp.where(odd, jnp.exp(first), 1.0)
    other_first = jnp.where(odd, 1.0, jnp.exp(fourth))
    other_second = jnp.where(odd, jnp.exp(third), 1.0)
    from_own = jnp.where(late, 1.0, jnp.exp(other))
    from_other = jnp.where(late, jnp.exp(own), 1.0)
    reach = jnp.exp(before)
    total = own + other
    for head in range(heads):
        rows, row = head_rows(head), slice(head, head + 1)
        one = got_one[rows].astype(F32)
        pair = own_first[row] * state_ref[rows] + own_second[row] * one
        far = other_first[row] * got_two[rows].astype(F32)
        far = far + other_second[row] * got_three[rows].astype(F32)
        low_ref[rows] = jnp.where(odd, one, 0.0).astype(BF16)
        high_ref[rows] = jnp.where(late, reach[row] * far, 0.0).astype(BF16)
        group = from_own[row] * pair + from_other[row] * far
        pay_ref[rows] = group.astype(BF16)
        if group_refs:
            group_refs[0][rows] = group
    pay_ref[width:] = packed_tail(total)
    before_ref[...] = jnp.where(late, before + other, before)
    if group_refs:
        group_refs[1][...] = total


def packed_tail(decay):
    heads = decay.shape[0]
    first, second = split(decay)
    third = (decay - first.astype(F32) - second.astype(F32)).astype(BF16)
    terms = [first.astype(F32), second.astype(F32), third.astype(F32)]
    terms += [jnp.zeros_like(decay)] * (tail_rows(heads) // heads - 3)
    return jnp.concatenate(terms, axis=0).astype(BF16)


def near_levels(where, gots, state, decay, with_group):
    width, states = state.shape
    own = lambda dtype: pltpu.VMEM((width, states), dtype)
    row = pltpu.VMEM(decay.shape, F32)
    shapes = [own(BF16), own(BF16), pltpu.VMEM(gots[0].shape, BF16), row]
    if with_group:
        shapes += [own(F32), row]
    return pl.pallas_call(
        near_kernel,
        in_specs=[pl.BlockSpec(memory_space=pltpu.SMEM)]
        + [pl.BlockSpec(memory_space=pltpu.VMEM)] * 5,
        out_specs=[pl.BlockSpec(memory_space=pltpu.VMEM)] * len(shapes),
        out_shape=shapes,
        compiler_params=pltpu.CompilerParams(vmem_limit_bytes=16 * MIB),
        name="near_levels",
    )(where, *in_vmem(*gots, state, decay))


def level_states(payload, state, decay, position, depth, beside):
    heads = decay.shape[0]
    gots = [flipped(payload, "ctx", mask) for mask in (1, 2, 3)]
    *gots, beside = lax.optimization_barrier((*gots, beside))
    where = position.astype(jnp.int32).reshape(1)
    low, high, payload, before, *group = near_levels(where, gots, state, decay, depth > 3)
    levels = [low, high]
    state, decay = group or (state, decay)
    for bit in range(2, depth):
        upper = ((position >> bit) & 1) == 1
        other, other_decay = unpacked(flipped(payload, "ctx", 1 << bit), heads)
        level, before = level_of(upper, before, other, other_decay)
        levels.append(level)
        if bit < depth - 1:
            state, decay = joined(upper, state, decay, other, other_decay)
            payload = packed(state, decay)
    return levels, beside


def silu(z):
    return z * (0.5 + 0.5 * jnp.tanh(0.5 * z))


def within_kernel(
    x_ref, z_ref, b_ref, c_ref, dt_ref, prefix_ref, state_ref, skip_ref, base_ref, gating_ref
):
    tokens, width = x_ref.shape
    heads = dt_ref.shape[0]
    skip = jnp.broadcast_to(as_column(skip_ref[...]), (heads, BLOCK))
    row = lax.broadcasted_iota(jnp.int32, (BLOCK, BLOCK), 0)
    col = lax.broadcasted_iota(jnp.int32, (BLOCK, BLOCK), 1)
    for block in range(tokens // BLOCK):
        part = slice(block * BLOCK, (block + 1) * BLOCK)
        prefix = prefix_ref[:, part]
        grow, shrink = jnp.exp(-prefix), jnp.exp(prefix)
        steps = dt_ref[:, part]
        readout = c_ref[part]
        scores = mm(b_ref[part], readout, TRANSPOSED_RHS)
        high, low = split(jnp.where(row <= col, scores, 0.0))
        turned = x_ref[part].T
        highs, lows = [], []
        for head in range(heads):
            x = turned[head_rows(head)].astype(F32)
            scaled = (x * steps[head:head + 1]).astype(BF16).astype(F32)
            weighted, rest = split(scaled * grow[head:head + 1])
            highs.append(weighted)
            lows.append(rest)
        weighted, rest = jnp.concatenate(highs, axis=0), jnp.concatenate(lows, axis=0)
        total = mm(
            jnp.concatenate([weighted, weighted, rest], axis=1),
            jnp.concatenate([high, low, high], axis=0),
        ) + mm(state_ref[block], readout, TRANSPOSED_RHS)
        z_turned = z_ref[part].T
        gating_ref[:, part] = z_turned
        for head in range(heads):
            rows = head_rows(head)
            x = turned[rows].astype(F32)
            mixed = total[rows] * shrink[head:head + 1] + skip[head:head + 1] * x
            base_ref[rows, part] = (mixed * silu(z_turned[rows].astype(F32))).astype(BF16)


def within_blocks(entries, gating, state_in, state_out, step_size, prefix, states, skip, tile=512):
    length, width = entries.shape
    heads = skip.shape[1]
    state = state_in.shape[1]
    tile = min(tile, length)
    by_rows = lambda cols: pl.BlockSpec((tile, cols), lambda i: (i, 0))
    by_cols = lambda rows: pl.BlockSpec((rows, tile), lambda i: (0, i))
    return pl.pallas_call(
        within_kernel,
        grid=(length // tile,),
        in_specs=[
            by_rows(width),
            by_rows(width),
            by_rows(state),
            by_rows(state),
            by_cols(heads),
            by_cols(heads),
            pl.BlockSpec((tile // BLOCK, width, state), lambda i: (i, 0, 0)),
            pl.BlockSpec((1, heads), lambda i: (0, 0)),
        ],
        out_specs=[by_cols(width), by_cols(width)],
        out_shape=[
            pltpu.VMEM((width, length), BF16),
            pltpu.HBM((width, length), BF16),
        ],
        compiler_params=params(24),
        name="within_blocks",
    )(
        *in_hbm(entries, gating, state_in, state_out, step_size, prefix),
        *in_vmem(states),
        *in_hbm(skip),
    )


def across_kernel(depth, base_ref, z_ref, c_ref, gate_ref, cum_ref, *refs):
    level_refs, (gated_ref, sums_ref) = refs[:depth], refs[depth:]
    width, tokens = base_ref.shape
    heads = cum_ref.shape[0]
    per_pair = 128 // HEAD_DIM
    for block in range(tokens // BLOCK):
        part = slice(block * BLOCK, (block + 1) * BLOCK)
        decayed = jnp.exp(cum_ref[:, part])
        gates = [gate_ref[rung, :, part] * decayed for rung in range(depth)]
        readouts = [mm(level_ref[...], c_ref[part], TRANSPOSED_RHS) for level_ref in level_refs]
        squares = jnp.zeros((HEAD_DIM, BLOCK), F32)
        for first in range(0, heads, per_pair):
            pair = []
            for head in range(first, first + per_pair):
                rows = head_rows(head)
                total = jnp.zeros((HEAD_DIM, BLOCK), F32)
                for gate, readout in zip(gates, readouts):
                    total = total + readout[rows] * gate[head:head + 1]
                gated = base_ref[rows, part].astype(F32) + total * silu(z_ref[rows, part].astype(F32))
                squares = squares + gated * gated
                pair.append(gated)
            cols = slice(first * HEAD_DIM, (first + per_pair) * HEAD_DIM)
            gated_ref[part, cols] = jnp.concatenate(pair, axis=0).T.astype(BF16)
        sums_ref[:, part] = jnp.sum(squares, axis=0, keepdims=True)


def across_levels(base, gating, state_out, level_gate, cumulative, levels, tile=1024):
    width, length = base.shape
    rungs, heads = level_gate.shape[:2]
    state = state_out.shape[1]
    tile = min(tile, length)
    by_cols = lambda rows: pl.BlockSpec((rows, tile), lambda i: (0, i))
    return pl.pallas_call(
        functools.partial(across_kernel, len(levels)),
        grid=(length // tile,),
        in_specs=[
            by_cols(width),
            by_cols(width),
            pl.BlockSpec((tile, state), lambda i: (i, 0)),
            pl.BlockSpec((rungs, heads, tile), lambda i: (0, 0, i)),
            by_cols(heads),
        ]
        + [pl.BlockSpec((width, state), lambda i: (0, 0))] * len(levels),
        out_specs=[pl.BlockSpec((tile, width), lambda i: (i, 0)), by_cols(1)],
        out_shape=[
            pltpu.VMEM((length, width), BF16),
            jax.ShapeDtypeStruct((1, length), F32),
        ],
        compiler_params=params(24),
        name="across_levels",
    )(
        *in_vmem(base),
        *in_hbm(gating, state_out, level_gate, cumulative),
        *levels,
    )


def normalize(channels, gated_ref, sums_ref, gain_ref, normed_ref):
    for block in range(gated_ref.shape[0] // BLOCK):
        part = slice(block * BLOCK, (block + 1) * BLOCK)
        inverse = lax.rsqrt(jnp.sum(sums_ref[:, part], axis=0, keepdims=True) / channels + 1e-05)
        column = jnp.broadcast_to(inverse, (8, BLOCK)).T[:, 0:1]
        normed_ref[part] = (gated_ref[part].astype(F32) * column * gain_ref[...]).astype(BF16)


def gradient_kernel(channels, gated_ref, sums_ref, gain_ref, cot_ref, normed_ref, out_ref):
    @pl.when(pl.program_id(0) == 0)
    def _():
        normalize(channels, gated_ref, sums_ref, gain_ref, normed_ref)

    out_ref[...] = mm(cot_ref[...], normed_ref[...], TRANSPOSED_LHS)


def norm_gradient(gated, sums, gain, cotangent, channels, tile=512):
    length, width = gated.shape
    rows = cotangent.shape[1]
    whole = lambda shape: pl.BlockSpec(shape, lambda i: (0,) * len(shape))
    return pl.pallas_call(
        functools.partial(gradient_kernel, channels),
        grid=(rows // tile,),
        in_specs=[
            whole((length, width)),
            whole(sums.shape),
            whole((1, width)),
            pl.BlockSpec((length, tile), lambda i: (0, i)),
        ],
        out_specs=[whole((length, width)), pl.BlockSpec((tile, width), lambda i: (i, 0))],
        out_shape=[
            jax.ShapeDtypeStruct((length, width), BF16),
            jax.ShapeDtypeStruct((rows, width), F32),
        ],
        compiler_params=params(32),
        name="norm_gradient",
    )(*in_vmem(gated), sums, gain, *in_hbm(cotangent))


def masks_of(bits):
    masks = [0]
    for bit in reversed(bits):
        masks = masks + [mask | 1 << bit for mask in masks]
    return masks


def slot_flips(order, kind, keep):
    later = masks_of(order[2:])
    later = later[:1] if kind == "near" else later[1:]
    first = 0 if keep else 1 << order[0]
    return [first | second | mask for second in (0, 1 << order[1]) for mask in later]


def column_specs(orders, jobs, tile, chunk):
    def spec(flip, half):
        return pl.BlockSpec(
            (tile, chunk), lambda i, pos_ref: (i, 2 * (pos_ref[0] ^ flip) + half)
        )

    return [
        spec(flip, half)
        for kind, keep in jobs
        for half, order in enumerate(orders)
        for flip in slot_flips(order, kind, keep)
    ]


def terms_kernel(channels, pos_ref, *refs):
    refs, acc_ref = refs[:-1], refs[-1]
    if channels is None:
        normed_ref, rest = refs[0], refs[1:]
    else:
        gated_ref, sums_ref, gain_ref, *rest = refs
    outs = [ref for ref in rest if len(ref.shape) == 3]
    rest = [ref for ref in rest if len(ref.shape) == 2]
    if channels is not None:
        normed_ref = rest.pop()
        normalize(channels, gated_ref, sums_ref, gain_ref, normed_ref)
    columns = jnp.concatenate([ref[...] for ref in rest], axis=1)
    product = mm(columns, normed_ref[...], TRANSPOSED_LHS)
    step, steps = pl.program_id(0), pl.num_programs(0)

    @pl.when(step == 0)
    def _():
        acc_ref[...] = product

    @pl.when((step > 0) & (step < steps - 1))
    def _():
        acc_ref[...] += product

    @pl.when(step == steps - 1)
    def _():
        start = 0
        for out_ref in outs:
            slots, chunk, _ = out_ref.shape
            rows = slice(start, start + slots * chunk)
            total = acc_ref[rows] + product[rows]
            out_ref[...] = total.reshape(out_ref.shape).astype(out_ref.dtype)
            start += slots * chunk


def terms_call(name, position, normed, cotangent, orders, jobs, chunk, norm=None, tile=1024):
    length, width = cotangent.shape[0], normed.shape[1]
    tile = min(tile, length // 2)
    cots = column_specs(orders, jobs, tile, chunk)
    shapes = [
        (len(slot_flips(order, kind, keep)), chunk, width)
        for kind, keep in jobs
        for order in orders
    ]
    dtypes = [F32 if keep else BF16 for _, keep in jobs for _ in orders]
    whole = lambda shape: pl.BlockSpec(shape, lambda i, pos_ref: (0,) * len(shape))
    by_tokens = pl.BlockSpec((tile, width), lambda i, pos_ref: (i, 0))
    in_specs, outs, out_specs, channels = [by_tokens], [], [], None
    if norm is None:
        inputs = in_hbm(normed)
    else:
        sums, gain, channels = norm
        inputs = [*in_vmem(normed), sums, gain]
        in_specs += [
            pl.BlockSpec((sums.shape[0], tile), lambda i, pos_ref: (0, i)),
            whole(gain.shape),
        ]
        outs, out_specs = [pltpu.HBM(normed.shape, BF16)], [by_tokens]
    result = pl.pallas_call(
        functools.partial(terms_kernel, channels),
        grid_spec=pltpu.PrefetchScalarGridSpec(
            num_scalar_prefetch=1,
            grid=(length // tile,),
            in_specs=in_specs + cots,
            out_specs=out_specs + [whole(shape) for shape in shapes],
            scratch_shapes=[pltpu.VMEM((len(cots) * chunk, width), F32)],
        ),
        out_shape=outs + [jax.ShapeDtypeStruct(*each) for each in zip(shapes, dtypes)],
        compiler_params=params(32),
        name=name,
    )(position, *inputs, *in_hbm(*[cotangent] * len(cots)))
    terms = result[len(outs):]
    return result[:len(outs)], [terms[2 * job:2 * job + 2] for job in range(len(jobs))]


def place_kernel(slots, rows, pos_ref, *refs):
    block_refs, (out_ref, sems) = refs[:len(slots)], refs[-2:]
    copies = []
    for block_ref, (masks, half) in zip(block_refs, slots):
        _, chunk, _ = block_ref.shape
        for slot, mask in enumerate(masks):
            row = pl.multiple_of((pos_ref[0] ^ mask) * rows + half * chunk, chunk)
            copies.append(
                pltpu.make_async_copy(
                    block_ref.at[slot], out_ref.at[pl.ds(row, chunk)], sems.at[len(copies)]
                )
            )
    for copy in copies:
        copy.start()
    for copy in copies:
        copy.wait()


def placed(position, pieces, shape, rows, name, already=None):
    blocks = [block for block, *_ in pieces]
    slots = [tuple(place) for _, *place in pieces]
    before = [] if already is None else [already]
    return pl.pallas_call(
        functools.partial(place_kernel, slots, rows),
        in_specs=[pl.BlockSpec(memory_space=pltpu.SMEM)]
        + [pl.BlockSpec(memory_space=pltpu.VMEM)] * len(blocks)
        + [pl.BlockSpec(memory_space=pltpu.HBM)] * len(before),
        out_specs=pl.BlockSpec(memory_space=pltpu.HBM),
        out_shape=pltpu.HBM(shape, BF16),
        scratch_shapes=[pltpu.SemaphoreType.DMA((sum(len(masks) for masks, *_ in slots),))],
        input_output_aliases={1 + len(blocks): 0} if before else {},
        compiler_params=pltpu.CompilerParams(vmem_limit_bytes=16 * MIB),
        name=name,
    )(position, *blocks, *before)


def adamw(gradient, master, moment_one, moment_two):
    moment_one = 0.9 * moment_one + 0.1 * gradient
    moment_two = 0.95 * moment_two + 0.05 * gradient * gradient
    ratio = moment_one / (1.0 - 0.9**10) / (jnp.sqrt(moment_two / (1.0 - 0.95**10)) + 1e-08)
    return (master - 0.1 * (ratio + 0.1 * master)).astype(BF16)


def update_kernel(keep_ref, got_ref, master_ref, one_ref, two_ref, gradient_ref, updated_ref):
    gradient = keep_ref[...] + got_ref[...].astype(F32)
    gradient_ref[...] = gradient
    updated_ref[...] = adamw(gradient, master_ref[...], one_ref[...], two_ref[...])


def update(keep, got, master, one, two):
    shape = keep.shape
    return pl.pallas_call(
        update_kernel,
        out_shape=[pltpu.VMEM(shape, F32), pltpu.VMEM(shape, BF16)],
        compiler_params=pltpu.CompilerParams(vmem_limit_bytes=16 * MIB),
        name="update_rows",
    )(keep, got, master, one, two)


def flipped(block, axis, mask):
    count = lax.axis_size(axis)
    return lax.ppermute(block, axis, [(i, i ^ mask) for i in range(count)])


def first_sums(keeps, sends, orders):
    sums = []
    for keep, send, order in zip(keeps, sends, orders):
        total = keep + flipped(send, "ctx", 1 << order[0]).astype(F32)
        slots = total.shape[0] // 2
        sums.append((total[slots:].astype(BF16), total[:slots]))
    return sums


def second_sums(sums, orders):
    halves = [
        keep + flipped(send, "ctx", 1 << order[1]).astype(F32)
        for (send, keep), order in zip(sums, orders)
    ]
    return jnp.concatenate(halves, axis=1)


def nearby(have, orders):
    chunk = have.shape[1] // 2
    halves = []
    for half, order in enumerate(orders):
        mine = have[:, half * chunk:(half + 1) * chunk]
        halves.append(jnp.concatenate([mine, flipped(mine, "ctx", 1 << order[1])], axis=0))
    return halves


def gathered(halves, masks, orders):
    pieces = []
    for half, order in enumerate(orders):
        names = masks + [mask | 1 << order[1] for mask in masks]
        last = flipped(halves[half], "ctx", 1 << order[0])
        pieces.append((halves[half], names, half))
        pieces.append((last, [mask | 1 << order[0] for mask in names], half))
    return pieces


def on_device(
    entries,
    gating,
    state_in,
    state_out,
    step_size,
    decay_rate,
    skip_gain,
    level_gate,
    norm_gain,
    cotangent,
    master_weight,
    first_moment,
    second_moment,
):
    width = entries.shape[1]
    channels = width * lax.axis_size("head")
    count = lax.axis_size("ctx")
    depth = count.bit_length() - 1
    position = lax.axis_index("ctx")
    before_block, prefix, cumulative, group, decay, payload = segment_states(
        entries, state_in, step_size, decay_rate[None, :]
    )
    base, turned = within_blocks(
        entries, gating, state_in, state_out, step_size, prefix, before_block, skip_gain[None, :]
    )
    levels, (base, turned) = level_states(
        payload, group, decay, position, depth, (base, turned)
    )
    gates = level_gate.transpose(1, 0, 2)
    gated, sums = across_levels(base, turned, state_out, gates, cumulative, levels)
    sums = lax.all_gather(sums[0], "head", axis=0, tiled=False)

    rows = master_weight.shape[0]
    chunk = rows // 2
    gain = norm_gain[None, :]
    bits = list(range(depth))
    orders = [bits, [1, 0] + bits[2:]]
    where = position.astype(jnp.int32).reshape(1)
    if chunk % 128 == 0:
        call = lambda name, normed, jobs, **kw: terms_call(
            name, where, normed, cotangent, orders, jobs, chunk, **kw
        )
        (normed,), (far_sends,) = call(
            "far_terms_to_send", gated, [("far", False)], norm=(sums, gain, channels)
        )
        _, (far_keeps, near_sends) = call(
            "far_terms_to_keep", normed, [("far", True), ("near", False)]
        )
        firsts = first_sums(far_keeps, far_sends, orders)
        firsts, near_sends = lax.optimization_barrier((firsts, near_sends))
        far = second_sums(firsts, orders)
        far, again = lax.optimization_barrier((far, normed))
        _, (near_keeps,) = call("near_terms_to_keep", again, [("near", True)])
    else:
        normed, terms = norm_gradient(gated, sums, gain, cotangent, channels)
        terms = terms.reshape(count, 2, chunk, width)
        pick = lambda kind, keep: [
            terms[position ^ jnp.array(slot_flips(order, kind, keep)), half].astype(
                F32 if keep else BF16
            )
            for half, order in enumerate(orders)
        ]
        far_sends, far_keeps = pick("far", False), pick("far", True)
        near_sends, near_keeps = pick("near", False), pick("near", True)
        far = second_sums(first_sums(far_keeps, far_sends, orders), orders)
    near = second_sums(first_sums(near_keeps, near_sends, orders), orders)
    totals = dict(zip(masks_of(bits[2:]), [near[0], *far]))
    for bit in bits[2:]:
        left = [mask for mask in totals if not mask >> bit & 1]
        send = jnp.stack([totals[mask | 1 << bit].astype(BF16) for mask in left])
        got = flipped(send, "ctx", 1 << bit)
        if bit == depth - 1:
            gradient, updated = update(
                totals[0], got[0], master_weight, first_moment, second_moment
            )
        totals = {mask: totals[mask] + got[at].astype(F32) for at, mask in enumerate(left)}
    halves = nearby(updated[None], orders)
    have, masks = updated[None], [0]
    for bit in reversed(bits[2:]):
        got = flipped(have, "ctx", 1 << bit)
        got = lax.optimization_barrier((got, halves[1]))[0]
        have = jnp.concatenate([have, got], axis=0)
        masks = masks + [mask | 1 << bit for mask in masks]
    far_blocks, *halves = lax.optimization_barrier((have[1:], *halves))
    pieces = gathered(halves, [0], orders)
    pieces += gathered(nearby(far_blocks, orders), masks[1:], orders)
    shape = (count * rows, width)
    late = [pieces[5], pieces[7]]
    early = pieces[:5] + [pieces[6]]
    weights = placed(where, early, shape, rows, "placed_early")
    weights = placed(where, late, shape, rows, "placed_late", weights)
    return (normed, weights, gradient)


def solution(mesh):
    return jax.shard_map(
        on_device,
        mesh=mesh,
        in_specs=(
            P("ctx", "head"),
            P("ctx", "head"),
            P("ctx", None),
            P("ctx", None),
            P("head", "ctx"),
            P("head"),
            P("head"),
            P("head", None, "ctx"),
            P("head"),
            P("ctx", None),
            P("ctx", "head"),
            P("ctx", "head"),
            P("ctx", "head"),
        ),
        out_specs=(P("ctx", "head"), P(None, "head"), P("ctx", "head")),
        check_vma=False,
    )
```

```python
import functools

import jax
import jax.numpy as jnp
from jax import lax
from jax.experimental import pallas as pl
from jax.experimental.pallas import tpu as pltpu
from jax.sharding import PartitionSpec as P

HEAD_DIM = 64
BLOCK = 256
BF16 = jnp.bfloat16
F32 = jnp.float32
MIB = 1024 * 1024
TRANSPOSED_LHS = (((0,), (0,)), ((), ()))
TRANSPOSED_RHS = (((1,), (1,)), ((), ()))


def mm(a, b, dims=(((1,), (0,)), ((), ()))):
    return lax.dot_general(a, b, dims, preferred_element_type=F32)


def split(values):
    high = values.astype(BF16)
    return high, (values - high.astype(F32)).astype(BF16)


def params(mib, steps=1):
    return pltpu.CompilerParams(
        dimension_semantics=("arbitrary",) * steps, vmem_limit_bytes=mib * MIB
    )


def in_hbm(*arrays):
    return [pltpu.with_memory_space_constraint(array, pltpu.HBM) for array in arrays]


def in_vmem(*arrays):
    return [pltpu.with_memory_space_constraint(array, pltpu.VMEM) for array in arrays]


def turn_blocks(values):
    blocks = values.shape[1] // BLOCK
    return jnp.concatenate([values[:, i * BLOCK:(i + 1) * BLOCK] for i in range(blocks)], axis=0)


def prefix_sums(values):
    heads, tokens = values.shape
    rows = turn_blocks(values)
    row = lax.broadcasted_iota(jnp.int32, (BLOCK, BLOCK), 0)
    col = lax.broadcasted_iota(jnp.int32, (BLOCK, BLOCK), 1)
    upper = jnp.where(row <= col, 1.0, 0.0).astype(BF16)
    first, rest = split(rows)
    last = (rows - first.astype(F32) - rest.astype(F32)).astype(BF16)
    sums = mm(jnp.concatenate([first, rest, last], axis=0), upper)
    count = rows.shape[0]
    sums = sums[0:count] + sums[count:2 * count] + sums[2 * count:3 * count]
    return [sums[i * heads:(i + 1) * heads] for i in range(tokens // BLOCK)]


def as_column(row):
    heads = row.shape[1]
    diagonal = lax.broadcasted_iota(jnp.int32, (heads, heads), 0) == lax.broadcasted_iota(
        jnp.int32, (heads, heads), 1
    )
    return jnp.sum(jnp.where(diagonal, row, 0.0), axis=1, keepdims=True)


def head_rows(head):
    return slice(head * HEAD_DIM, (head + 1) * HEAD_DIM)


def states_kernel(
    x_ref, b_ref, dt_ref, rate_ref, before_ref, prefix_ref, cum_ref, end_ref, decay_ref, pay_ref,
    run_ref, off_ref
):
    step = pl.program_id(0)
    tokens, width = x_ref.shape
    states = b_ref.shape[1]
    heads = dt_ref.shape[0]

    @pl.when(step == 0)
    def _():
        run_ref[...] = jnp.zeros_like(run_ref)
        off_ref[...] = jnp.zeros_like(off_ref)

    offset = off_ref[:, 0:1]
    rate = as_column(rate_ref[...])
    for block, prefix in enumerate(prefix_sums(-rate * dt_ref[...])):
        part = slice(block * BLOCK, (block + 1) * BLOCK)
        prefix_ref[:, part] = prefix
        cum_ref[:, part] = prefix + offset
        last = prefix[:, BLOCK - 1:BLOCK]
        weight = jnp.exp(last - prefix)
        decay = jnp.broadcast_to(jnp.exp(last), (heads, states))
        steps = dt_ref[:, part]
        turned = x_ref[part].T
        pieces = []
        for head in range(heads):
            x = turned[head_rows(head)].astype(F32)
            scaled = (x * steps[head:head + 1]).astype(BF16).astype(F32)
            pieces.append((scaled * weight[head:head + 1]).astype(BF16))
        update = mm(jnp.concatenate(pieces, axis=0), b_ref[part])
        for head in range(heads):
            rows = head_rows(head)
            running = run_ref[rows]
            before_ref[block, rows] = running.astype(BF16)
            run_ref[rows] = decay[head:head + 1] * running + update[rows]
        offset = offset + last
    off_ref[...] = jnp.broadcast_to(offset, off_ref.shape)

    @pl.when(step == pl.num_programs(0) - 1)
    def _():
        total = jnp.broadcast_to(offset, (heads, states))
        end_ref[...] = run_ref[...]
        decay_ref[...] = total
        pay_ref[0:width] = run_ref[...].astype(BF16)
        pay_ref[width:] = packed_tail(total)


def tail_rows(heads):
    return -(-3 * heads // 16) * 16


def segment_states(entries, state_in, step_size, rate, tile=1024):
    length, width = entries.shape
    heads = rate.shape[1]
    states = state_in.shape[1]
    tile = min(tile, length)
    whole = lambda shape: pl.BlockSpec(shape, lambda i: (0,) * len(shape))
    return pl.pallas_call(
        states_kernel,
        grid=(length // tile,),
        in_specs=[
            pl.BlockSpec((tile, width), lambda i: (i, 0)),
            pl.BlockSpec((tile, states), lambda i: (i, 0)),
            pl.BlockSpec((heads, tile), lambda i: (0, i)),
            whole((1, heads)),
        ],
        out_specs=[
            pl.BlockSpec((tile // BLOCK, width, states), lambda i: (i, 0, 0)),
            pl.BlockSpec((heads, tile), lambda i: (0, i)),
            pl.BlockSpec((heads, tile), lambda i: (0, i)),
            whole((width, states)),
            whole((heads, states)),
            whole((width + tail_rows(heads), states)),
        ],
        out_shape=[
            pltpu.VMEM((length // BLOCK, width, states), BF16),
            pltpu.HBM((heads, length), F32),
            pltpu.HBM((heads, length), F32),
            jax.ShapeDtypeStruct((width, states), F32),
            jax.ShapeDtypeStruct((heads, states), F32),
            pltpu.VMEM((width + tail_rows(heads), states), BF16),
        ],
        scratch_shapes=[pltpu.VMEM((width, states), F32), pltpu.VMEM((heads, 128), F32)],
        compiler_params=params(24),
        name="segment_states",
    )(*in_hbm(entries, state_in, step_size, rate))


def packed(state, decay):
    heads = decay.shape[0]
    first, second = split(decay)
    third = (decay - first.astype(F32) - second.astype(F32)).astype(BF16)
    spare = jnp.zeros((tail_rows(heads) - 3 * heads, decay.shape[1]), BF16)
    return jnp.concatenate([state.astype(BF16), first, second, third, spare], axis=0)


def unpacked(got, heads):
    width = got.shape[0] - tail_rows(heads)
    terms = got[width:width + 3 * heads].astype(F32).reshape(3, heads, got.shape[1])
    return got[0:width].astype(F32), terms[0] + terms[1] + terms[2]


def decayed(decay, state):
    heads, states = decay.shape
    return (jnp.exp(decay)[:, None, :] * state.reshape(heads, -1, states)).reshape(state.shape)


def joined(upper, state, decay, other, other_decay):
    both = jnp.where(
        upper, state + decayed(decay, other), other + decayed(other_decay, state)
    )
    return both, decay + other_decay


def level_of(upper, before, other, other_decay):
    level = jnp.where(upper, decayed(before, other), 0.0).astype(BF16)
    return level, jnp.where(upper, before + other_decay, before)


def near_kernel(
    pos_ref, got_one, got_two, got_three, state_ref, decay_ref,
    low_ref, high_ref, pay_ref, before_ref, *group_refs
):
    heads = decay_ref.shape[0]
    width = state_ref.shape[0]
    odd = (pos_ref[0] & 1) == 1
    late = ((pos_ref[0] >> 1) & 1) == 1
    first = decay_ref[...]

    def tail(got):
        terms = got[width:].astype(F32)
        return terms[0:heads] + terms[heads:2 * heads] + terms[2 * heads:3 * heads]

    second, third, fourth = tail(got_one), tail(got_two), tail(got_three)
    before = jnp.where(odd, second, 0.0)
    own, other = first + second, third + fourth
    own_first = jnp.where(odd, 1.0, jnp.exp(second))
    own_second = jnp.where(odd, jnp.exp(first), 1.0)
    other_first = jnp.where(odd, 1.0, jnp.exp(fourth))
    other_second = jnp.where(odd, jnp.exp(third), 1.0)
    from_own = jnp.where(late, 1.0, jnp.exp(other))
    from_other = jnp.where(late, jnp.exp(own), 1.0)
    reach = jnp.exp(before)
    total = own + other
    for head in range(heads):
        rows, row = head_rows(head), slice(head, head + 1)
        one = got_one[rows].astype(F32)
        pair = own_first[row] * state_ref[rows] + own_second[row] * one
        far = other_first[row] * got_two[rows].astype(F32)
        far = far + other_second[row] * got_three[rows].astype(F32)
        low_ref[rows] = jnp.where(odd, one, 0.0).astype(BF16)
        high_ref[rows] = jnp.where(late, reach[row] * far, 0.0).astype(BF16)
        group = from_own[row] * pair + from_other[row] * far
        pay_ref[rows] = group.astype(BF16)
        if group_refs:
            group_refs[0][rows] = group
    pay_ref[width:] = packed_tail(total)
    before_ref[...] = jnp.where(late, before + other, before)
    if group_refs:
        group_refs[1][...] = total


def packed_tail(decay):
    heads = decay.shape[0]
    first, second = split(decay)
    third = (decay - first.astype(F32) - second.astype(F32)).astype(BF16)
    terms = [first.astype(F32), second.astype(F32), third.astype(F32)]
    terms += [jnp.zeros_like(decay)] * (tail_rows(heads) // heads - 3)
    return jnp.concatenate(terms, axis=0).astype(BF16)


def near_levels(where, gots, state, decay, with_group):
    width, states = state.shape
    own = lambda dtype: pltpu.VMEM((width, states), dtype)
    row = pltpu.VMEM(decay.shape, F32)
    shapes = [own(BF16), own(BF16), pltpu.VMEM(gots[0].shape, BF16), row]
    if with_group:
        shapes += [own(F32), row]
    return pl.pallas_call(
        near_kernel,
        in_specs=[pl.BlockSpec(memory_space=pltpu.SMEM)]
        + [pl.BlockSpec(memory_space=pltpu.VMEM)] * 5,
        out_specs=[pl.BlockSpec(memory_space=pltpu.VMEM)] * len(shapes),
        out_shape=shapes,
        compiler_params=pltpu.CompilerParams(vmem_limit_bytes=16 * MIB),
        name="near_levels",
    )(where, *in_vmem(*gots, state, decay))


def level_states(payload, state, decay, position, depth, beside):
    heads = decay.shape[0]
    gots = [flipped(payload, "ctx", mask) for mask in (1, 2, 3)]
    *gots, beside = lax.optimization_barrier((*gots, beside))
    where = position.astype(jnp.int32).reshape(1)
    low, high, payload, before, *group = near_levels(where, gots, state, decay, depth > 3)
    levels = [low, high]
    state, decay = group or (state, decay)
    for bit in range(2, depth):
        upper = ((position >> bit) & 1) == 1
        other, other_decay = unpacked(flipped(payload, "ctx", 1 << bit), heads)
        level, before = level_of(upper, before, other, other_decay)
        levels.append(level)
        if bit < depth - 1:
            state, decay = joined(upper, state, decay, other, other_decay)
            payload = packed(state, decay)
    return levels, beside


def silu(z):
    return z * (0.5 + 0.5 * jnp.tanh(0.5 * z))


def within_kernel(
    x_ref, z_ref, b_ref, c_ref, dt_ref, prefix_ref, state_ref, skip_ref, base_ref, gating_ref
):
    tokens, width = x_ref.shape
    heads = dt_ref.shape[0]
    skip = jnp.broadcast_to(as_column(skip_ref[...]), (heads, BLOCK))
    row = lax.broadcasted_iota(jnp.int32, (BLOCK, BLOCK), 0)
    col = lax.broadcasted_iota(jnp.int32, (BLOCK, BLOCK), 1)
    for block in range(tokens // BLOCK):
        part = slice(block * BLOCK, (block + 1) * BLOCK)
        prefix = prefix_ref[:, part]
        grow, shrink = jnp.exp(-prefix), jnp.exp(prefix)
        steps = dt_ref[:, part]
        readout = c_ref[part]
        scores = mm(b_ref[part], readout, TRANSPOSED_RHS)
        high, low = split(jnp.where(row <= col, scores, 0.0))
        turned = x_ref[part].T
        highs, lows = [], []
        for head in range(heads):
            x = turned[head_rows(head)].astype(F32)
            scaled = (x * steps[head:head + 1]).astype(BF16).astype(F32)
            weighted, rest = split(scaled * grow[head:head + 1])
            highs.append(weighted)
            lows.append(rest)
        weighted, rest = jnp.concatenate(highs, axis=0), jnp.concatenate(lows, axis=0)
        total = mm(
            jnp.concatenate([weighted, rest], axis=1),
            jnp.concatenate([high, high], axis=0),
        ) + mm(state_ref[block], readout, TRANSPOSED_RHS)
        z_turned = z_ref[part].T
        gating_ref[:, part] = z_turned
        for head in range(heads):
            rows = head_rows(head)
            x = turned[rows].astype(F32)
            mixed = total[rows] * shrink[head:head + 1] + skip[head:head + 1] * x
            base_ref[rows, part] = (mixed * silu(z_turned[rows].astype(F32))).astype(BF16)


def within_blocks(entries, gating, state_in, state_out, step_size, prefix, states, skip, tile=512):
    length, width = entries.shape
    heads = skip.shape[1]
    state = state_in.shape[1]
    tile = min(tile, length)
    by_rows = lambda cols: pl.BlockSpec((tile, cols), lambda i: (i, 0))
    by_cols = lambda rows: pl.BlockSpec((rows, tile), lambda i: (0, i))
    return pl.pallas_call(
        within_kernel,
        grid=(length // tile,),
        in_specs=[
            by_rows(width),
            by_rows(width),
            by_rows(state),
            by_rows(state),
            by_cols(heads),
            by_cols(heads),
            pl.BlockSpec((tile // BLOCK, width, state), lambda i: (i, 0, 0)),
            pl.BlockSpec((1, heads), lambda i: (0, 0)),
        ],
        out_specs=[by_cols(width), by_cols(width)],
        out_shape=[
            pltpu.VMEM((width, length), BF16),
            pltpu.HBM((width, length), BF16),
        ],
        compiler_params=params(24),
        name="within_blocks",
    )(
        *in_hbm(entries, gating, state_in, state_out, step_size, prefix),
        *in_vmem(states),
        *in_hbm(skip),
    )


def across_kernel(depth, base_ref, z_ref, c_ref, gate_ref, cum_ref, *refs):
    level_refs, (gated_ref, sums_ref) = refs[:depth], refs[depth:]
    width, tokens = base_ref.shape
    heads = cum_ref.shape[0]
    per_pair = 128 // HEAD_DIM
    for block in range(tokens // BLOCK):
        part = slice(block * BLOCK, (block + 1) * BLOCK)
        decayed = jnp.exp(cum_ref[:, part])
        gates = [gate_ref[rung, :, part] * decayed for rung in range(depth)]
        readouts = [mm(level_ref[...], c_ref[part], TRANSPOSED_RHS) for level_ref in level_refs]
        squares = jnp.zeros((HEAD_DIM, BLOCK), F32)
        for first in range(0, heads, per_pair):
            pair = []
            for head in range(first, first + per_pair):
                rows = head_rows(head)
                total = jnp.zeros((HEAD_DIM, BLOCK), F32)
                for gate, readout in zip(gates, readouts):
                    total = total + readout[rows] * gate[head:head + 1]
                gated = base_ref[rows, part].astype(F32) + total * silu(z_ref[rows, part].astype(F32))
                squares = squares + gated * gated
                pair.append(gated)
            cols = slice(first * HEAD_DIM, (first + per_pair) * HEAD_DIM)
            gated_ref[part, cols] = jnp.concatenate(pair, axis=0).T.astype(BF16)
        sums_ref[:, part] = jnp.sum(squares, axis=0, keepdims=True)


def across_levels(base, gating, state_out, level_gate, cumulative, levels, tile=1024):
    width, length = base.shape
    rungs, heads = level_gate.shape[:2]
    state = state_out.shape[1]
    tile = min(tile, length)
    by_cols = lambda rows: pl.BlockSpec((rows, tile), lambda i: (0, i))
    return pl.pallas_call(
        functools.partial(across_kernel, len(levels)),
        grid=(length // tile,),
        in_specs=[
            by_cols(width),
            by_cols(width),
            pl.BlockSpec((tile, state), lambda i: (i, 0)),
            pl.BlockSpec((rungs, heads, tile), lambda i: (0, 0, i)),
            by_cols(heads),
        ]
        + [pl.BlockSpec((width, state), lambda i: (0, 0))] * len(levels),
        out_specs=[pl.BlockSpec((tile, width), lambda i: (i, 0)), by_cols(1)],
        out_shape=[
            pltpu.VMEM((length, width), BF16),
            jax.ShapeDtypeStruct((1, length), F32),
        ],
        compiler_params=params(24),
        name="across_levels",
    )(
        *in_vmem(base),
        *in_hbm(gating, state_out, level_gate, cumulative),
        *levels,
    )


def normalize(channels, gated_ref, sums_ref, gain_ref, normed_ref):
    for block in range(gated_ref.shape[0] // BLOCK):
        part = slice(block * BLOCK, (block + 1) * BLOCK)
        inverse = lax.rsqrt(jnp.sum(sums_ref[:, part], axis=0, keepdims=True) / channels + 1e-05)
        column = jnp.broadcast_to(inverse, (8, BLOCK)).T[:, 0:1]
        normed_ref[part] = (gated_ref[part].astype(F32) * column * gain_ref[...]).astype(BF16)


def gradient_kernel(channels, gated_ref, sums_ref, gain_ref, cot_ref, normed_ref, out_ref):
    @pl.when(pl.program_id(0) == 0)
    def _():
        normalize(channels, gated_ref, sums_ref, gain_ref, normed_ref)

    out_ref[...] = mm(cot_ref[...], normed_ref[...], TRANSPOSED_LHS)


def norm_gradient(gated, sums, gain, cotangent, channels, tile=512):
    length, width = gated.shape
    rows = cotangent.shape[1]
    whole = lambda shape: pl.BlockSpec(shape, lambda i: (0,) * len(shape))
    return pl.pallas_call(
        functools.partial(gradient_kernel, channels),
        grid=(rows // tile,),
        in_specs=[
            whole((length, width)),
            whole(sums.shape),
            whole((1, width)),
            pl.BlockSpec((length, tile), lambda i: (0, i)),
        ],
        out_specs=[whole((length, width)), pl.BlockSpec((tile, width), lambda i: (i, 0))],
        out_shape=[
            jax.ShapeDtypeStruct((length, width), BF16),
            jax.ShapeDtypeStruct((rows, width), F32),
        ],
        compiler_params=params(32),
        name="norm_gradient",
    )(*in_vmem(gated), sums, gain, *in_hbm(cotangent))


def masks_of(bits):
    masks = [0]
    for bit in reversed(bits):
        masks = masks + [mask | 1 << bit for mask in masks]
    return masks


def slot_flips(order, kind, keep):
    later = masks_of(order[2:])
    later = later[:1] if kind == "near" else later[1:]
    first = 0 if keep else 1 << order[0]
    return [first | second | mask for second in (0, 1 << order[1]) for mask in later]


def column_specs(orders, jobs, tile, chunk):
    def spec(flip, half):
        return pl.BlockSpec(
            (tile, chunk), lambda i, pos_ref: (i, 2 * (pos_ref[0] ^ flip) + half)
        )

    return [
        spec(flip, half)
        for kind, keep in jobs
        for half, order in enumerate(orders)
        for flip in slot_flips(order, kind, keep)
    ]


def terms_kernel(channels, pos_ref, *refs):
    refs, acc_ref = refs[:-1], refs[-1]
    if channels is None:
        normed_ref, rest = refs[0], refs[1:]
    else:
        gated_ref, sums_ref, gain_ref, *rest = refs
    outs = [ref for ref in rest if len(ref.shape) == 3]
    rest = [ref for ref in rest if len(ref.shape) == 2]
    if channels is not None:
        normed_ref = rest.pop()
        normalize(channels, gated_ref, sums_ref, gain_ref, normed_ref)
    columns = jnp.concatenate([ref[...] for ref in rest], axis=1)
    product = mm(columns, normed_ref[...], TRANSPOSED_LHS)
    step, steps = pl.program_id(0), pl.num_programs(0)

    @pl.when(step == 0)
    def _():
        acc_ref[...] = product

    @pl.when((step > 0) & (step < steps - 1))
    def _():
        acc_ref[...] += product

    @pl.when(step == steps - 1)
    def _():
        start = 0
        for out_ref in outs:
            slots, chunk, _ = out_ref.shape
            rows = slice(start, start + slots * chunk)
            total = acc_ref[rows] + product[rows]
            out_ref[...] = total.reshape(out_ref.shape).astype(out_ref.dtype)
            start += slots * chunk


def terms_call(name, position, normed, cotangent, orders, jobs, chunk, norm=None, tile=1024):
    length, width = cotangent.shape[0], normed.shape[1]
    tile = min(tile, length // 2)
    cots = column_specs(orders, jobs, tile, chunk)
    shapes = [
        (len(slot_flips(order, kind, keep)), chunk, width)
        for kind, keep in jobs
        for order in orders
    ]
    dtypes = [F32 if keep else BF16 for _, keep in jobs for _ in orders]
    whole = lambda shape: pl.BlockSpec(shape, lambda i, pos_ref: (0,) * len(shape))
    by_tokens = pl.BlockSpec((tile, width), lambda i, pos_ref: (i, 0))
    in_specs, outs, out_specs, channels = [by_tokens], [], [], None
    if norm is None:
        inputs = in_hbm(normed)
    else:
        sums, gain, channels = norm
        inputs = [*in_vmem(normed), sums, gain]
        in_specs += [
            pl.BlockSpec((sums.shape[0], tile), lambda i, pos_ref: (0, i)),
            whole(gain.shape),
        ]
        outs, out_specs = [pltpu.HBM(normed.shape, BF16)], [by_tokens]
    result = pl.pallas_call(
        functools.partial(terms_kernel, channels),
        grid_spec=pltpu.PrefetchScalarGridSpec(
            num_scalar_prefetch=1,
            grid=(length // tile,),
            in_specs=in_specs + cots,
            out_specs=out_specs + [whole(shape) for shape in shapes],
            scratch_shapes=[pltpu.VMEM((len(cots) * chunk, width), F32)],
        ),
        out_shape=outs + [jax.ShapeDtypeStruct(*each) for each in zip(shapes, dtypes)],
        compiler_params=params(32),
        name=name,
    )(position, *inputs, *in_hbm(*[cotangent] * len(cots)))
    terms = result[len(outs):]
    return result[:len(outs)], [terms[2 * job:2 * job + 2] for job in range(len(jobs))]


def place_kernel(slots, rows, pos_ref, *refs):
    block_refs, (out_ref, sems) = refs[:len(slots)], refs[-2:]
    copies = []
    for block_ref, (masks, half) in zip(block_refs, slots):
        _, chunk, _ = block_ref.shape
        for slot, mask in enumerate(masks):
            row = pl.multiple_of((pos_ref[0] ^ mask) * rows + half * chunk, chunk)
            copies.append(
                pltpu.make_async_copy(
                    block_ref.at[slot], out_ref.at[pl.ds(row, chunk)], sems.at[len(copies)]
                )
            )
    for copy in copies:
        copy.start()
    for copy in copies:
        copy.wait()


def placed(position, pieces, shape, rows, name, already=None):
    blocks = [block for block, *_ in pieces]
    slots = [tuple(place) for _, *place in pieces]
    before = [] if already is None else [already]
    return pl.pallas_call(
        functools.partial(place_kernel, slots, rows),
        in_specs=[pl.BlockSpec(memory_space=pltpu.SMEM)]
        + [pl.BlockSpec(memory_space=pltpu.VMEM)] * len(blocks)
        + [pl.BlockSpec(memory_space=pltpu.HBM)] * len(before),
        out_specs=pl.BlockSpec(memory_space=pltpu.HBM),
        out_shape=pltpu.HBM(shape, BF16),
        scratch_shapes=[pltpu.SemaphoreType.DMA((sum(len(masks) for masks, *_ in slots),))],
        input_output_aliases={1 + len(blocks): 0} if before else {},
        compiler_params=pltpu.CompilerParams(vmem_limit_bytes=16 * MIB),
        name=name,
    )(position, *blocks, *before)


def adamw(gradient, master, moment_one, moment_two):
    moment_one = 0.9 * moment_one + 0.1 * gradient
    moment_two = 0.95 * moment_two + 0.05 * gradient * gradient
    ratio = moment_one / (1.0 - 0.9**10) / (jnp.sqrt(moment_two / (1.0 - 0.95**10)) + 1e-08)
    return (master - 0.1 * (ratio + 0.1 * master)).astype(BF16)


def update_kernel(keep_ref, got_ref, master_ref, one_ref, two_ref, gradient_ref, updated_ref):
    gradient = keep_ref[...] + got_ref[...].astype(F32)
    gradient_ref[...] = gradient
    updated_ref[...] = adamw(gradient, master_ref[...], one_ref[...], two_ref[...])


def update(keep, got, master, one, two):
    shape = keep.shape
    return pl.pallas_call(
        update_kernel,
        out_shape=[pltpu.VMEM(shape, F32), pltpu.VMEM(shape, BF16)],
        compiler_params=pltpu.CompilerParams(vmem_limit_bytes=16 * MIB),
        name="update_rows",
    )(keep, got, master, one, two)


def flipped(block, axis, mask):
    count = lax.axis_size(axis)
    return lax.ppermute(block, axis, [(i, i ^ mask) for i in range(count)])


def first_sums(keeps, sends, orders):
    sums = []
    for keep, send, order in zip(keeps, sends, orders):
        total = keep + flipped(send, "ctx", 1 << order[0]).astype(F32)
        slots = total.shape[0] // 2
        sums.append((total[slots:].astype(BF16), total[:slots]))
    return sums


def second_sums(sums, orders):
    halves = [
        keep + flipped(send, "ctx", 1 << order[1]).astype(F32)
        for (send, keep), order in zip(sums, orders)
    ]
    return jnp.concatenate(halves, axis=1)


def nearby(have, orders):
    chunk = have.shape[1] // 2
    halves = []
    for half, order in enumerate(orders):
        mine = have[:, half * chunk:(half + 1) * chunk]
        halves.append(jnp.concatenate([mine, flipped(mine, "ctx", 1 << order[1])], axis=0))
    return halves


def gathered(halves, masks, orders):
    pieces = []
    for half, order in enumerate(orders):
        names = masks + [mask | 1 << order[1] for mask in masks]
        last = flipped(halves[half], "ctx", 1 << order[0])
        pieces.append((halves[half], names, half))
        pieces.append((last, [mask | 1 << order[0] for mask in names], half))
    return pieces


def on_device(
    entries,
    gating,
    state_in,
    state_out,
    step_size,
    decay_rate,
    skip_gain,
    level_gate,
    norm_gain,
    cotangent,
    master_weight,
    first_moment,
    second_moment,
):
    width = entries.shape[1]
    channels = width * lax.axis_size("head")
    count = lax.axis_size("ctx")
    depth = count.bit_length() - 1
    position = lax.axis_index("ctx")
    before_block, prefix, cumulative, group, decay, payload = segment_states(
        entries, state_in, step_size, decay_rate[None, :]
    )
    base, turned = within_blocks(
        entries, gating, state_in, state_out, step_size, prefix, before_block, skip_gain[None, :]
    )
    levels, (base, turned) = level_states(
        payload, group, decay, position, depth, (base, turned)
    )
    gates = level_gate.transpose(1, 0, 2)
    gated, sums = across_levels(base, turned, state_out, gates, cumulative, levels)
    sums = lax.all_gather(sums[0], "head", axis=0, tiled=False)

    rows = master_weight.shape[0]
    chunk = rows // 2
    gain = norm_gain[None, :]
    bits = list(range(depth))
    orders = [bits, [1, 0] + bits[2:]]
    where = position.astype(jnp.int32).reshape(1)
    if chunk % 128 == 0:
        call = lambda name, normed, jobs, **kw: terms_call(
            name, where, normed, cotangent, orders, jobs, chunk, **kw
        )
        (normed,), (far_sends,) = call(
            "far_terms_to_send", gated, [("far", False)], norm=(sums, gain, channels)
        )
        _, (far_keeps, near_sends) = call(
            "far_terms_to_keep", normed, [("far", True), ("near", False)]
        )
        firsts = first_sums(far_keeps, far_sends, orders)
        firsts, near_sends = lax.optimization_barrier((firsts, near_sends))
        far = second_sums(firsts, orders)
        far, again = lax.optimization_barrier((far, normed))
        _, (near_keeps,) = call("near_terms_to_keep", again, [("near", True)])
    else:
        normed, terms = norm_gradient(gated, sums, gain, cotangent, channels)
        terms = terms.reshape(count, 2, chunk, width)
        pick = lambda kind, keep: [
            terms[position ^ jnp.array(slot_flips(order, kind, keep)), half].astype(
                F32 if keep else BF16
            )
            for half, order in enumerate(orders)
        ]
        far_sends, far_keeps = pick("far", False), pick("far", True)
        near_sends, near_keeps = pick("near", False), pick("near", True)
        far = second_sums(first_sums(far_keeps, far_sends, orders), orders)
    near = second_sums(first_sums(near_keeps, near_sends, orders), orders)
    totals = dict(zip(masks_of(bits[2:]), [near[0], *far]))
    for bit in bits[2:]:
        left = [mask for mask in totals if not mask >> bit & 1]
        send = jnp.stack([totals[mask | 1 << bit].astype(BF16) for mask in left])
        got = flipped(send, "ctx", 1 << bit)
        if bit == depth - 1:
            gradient, updated = update(
                totals[0], got[0], master_weight, first_moment, second_moment
            )
        totals = {mask: totals[mask] + got[at].astype(F32) for at, mask in enumerate(left)}
    halves = nearby(updated[None], orders)
    have, masks = updated[None], [0]
    for bit in reversed(bits[2:]):
        got = flipped(have, "ctx", 1 << bit)
        got = lax.optimization_barrier((got, halves[1]))[0]
        have = jnp.concatenate([have, got], axis=0)
        masks = masks + [mask | 1 << bit for mask in masks]
    far_blocks, *halves = lax.optimization_barrier((have[1:], *halves))
    pieces = gathered(halves, [0], orders)
    pieces += gathered(nearby(far_blocks, orders), masks[1:], orders)
    shape = (count * rows, width)
    late = [pieces[5], pieces[7]]
    early = pieces[:5] + [pieces[6]]
    weights = placed(where, early, shape, rows, "placed_early")
    weights = placed(where, late, shape, rows, "placed_late", weights)
    return (normed, weights, gradient)


def solution(mesh):
    return jax.shard_map(
        on_device,
        mesh=mesh,
        in_specs=(
            P("ctx", "head"),
            P("ctx", "head"),
            P("ctx", None),
            P("ctx", None),
            P("head", "ctx"),
            P("head"),
            P("head"),
            P("head", None, "ctx"),
            P("head"),
            P("ctx", None),
            P("ctx", "head"),
            P("ctx", "head"),
            P("ctx", "head"),
        ),
        out_specs=(P("ctx", "head"), P(None, "head"), P("ctx", "head")),
        check_vma=False,
    )
```
